32 devices in a mesh: edp: 2 (over core), ep: 16 (over z, y, x).
Axes of the slice: x: 2, y: 2, z: 4, core: 2. Of those that a mesh axis runs over, the one named last changes fastest.
Arguments:
- tokens: bfloat16 [4096, 3584], P(('edp', 'ep')), may hold values from -6 to 6
- cotangent: bfloat16 [4096, 3584], P(('edp', 'ep')), may hold values from -6 to 6
- expert_ids: int32 [4096, 8], P(('edp', 'ep')), may hold values from 0 to 383, as said below
- route_weight: float32 [4096, 8], P(('edp', 'ep')), may hold values from 0.1 to 0.7
- gate_weight: bfloat16 [16, 3584, 1024], P('ep', None, 'edp'), may hold values from -0.09375 to 0.09375
- up_weight: bfloat16 [16, 3584, 1024], P('ep', None, 'edp'), may hold values from -0.09375 to 0.09375
- down_weight: bfloat16 [16, 1024, 3584], P('ep', 'edp'), may hold values from -0.1875 to 0.1875
Outputs:
- routed_out: bfloat16 [4096, 3584], P(('edp', 'ep'))
- token_grad: bfloat16 [4096, 3584], P(('edp', 'ep'))
- grad_gate: bfloat16 [16, 3584, 1024], P('ep', None, 'edp')
- grad_up: bfloat16 [16, 3584, 1024], P('ep', None, 'edp')
- grad_down: bfloat16 [16, 1024, 3584], P('ep', 'edp')
The draws below stay inside these ranges and needn't reach their ends.
Inputs may be any that keep to these rules, and one draw needn't show every extreme that they name: `expert_ids`: each token names 8 different experts. Among the 128 tokens of one device (rows of one aligned block of 128) every expert is named by 2 to 4 tokens, and in every draw some expert below 16 is named by exactly 4 tokens of every device.
All inputs are finite; a program needn't handle non-finite values.
Results may differ from the reference program's by a relative error of at most 0.019.
Values may be sent and summed in bfloat16 or wider, within the bound.
No kernel may reach another device: no remote copies, remote signals or barrier semaphores. Data moves between devices by JAX's collectives and lax.ppermute only.
A program may use at most 128 MiB of HBM per device.

```python
import jax
import jax.numpy as jnp
from jax import lax

D = 3584
FF = 1024
EXPERTS_ALL = 384
TOP = 8
TOK_DEV = 128
CAP = 4
EXPERTS = 16
TOKENS = 4096
N_EDP = 2
N_EP = 16
DEVICES = 32


def draw_expert_ids(key, part):
    blocks = TOKENS // TOK_DEV
    unit_size = CAP // 4
    busiest = jax.random.randint(jax.random.fold_in(key, 11), (), 0, EXPERTS).astype(jnp.int32)

    def one_block(index):
        block_key = jax.random.fold_in(key, index)
        shift_key, order_key = jax.random.split(block_key)
        moved = jax.random.randint(shift_key, (), 0, 65).astype(jnp.int32)
        remaining = (jax.random.permutation(order_key, EXPERTS_ALL - 1) + 1).astype(jnp.int32)
        ordering = (busiest + jnp.concatenate([jnp.zeros((1,), jnp.int32), remaining])) % EXPERTS_ALL
        fours = 128 - moved
        threes = 2 * moved
        position = jnp.arange(TOK_DEV * TOP, dtype=jnp.int32) // unit_size
        edge_four = 4 * fours
        edge_three = edge_four + 3 * threes
        standing = jnp.where(position < edge_four, position // 4, jnp.where(position < edge_three, fours + (position - edge_four) // 3, fours + threes + (position - edge_three) // 2))
        return ordering[standing].reshape(TOP, TOK_DEV).T
    return jax.vmap(one_block)(jnp.arange(blocks, dtype=jnp.int32)).reshape(TOKENS, TOP).astype(jnp.int32)


def shard_levels(own_key, dims, pieces, low, high):
    def one(dim, parts):
        heights = jax.random.uniform(jax.random.fold_in(jax.random.fold_in(own_key, 6), dim), (parts,), jnp.float32, low / len(pieces), high / len(pieces))
        return jnp.repeat(jnp.exp(heights), dims[dim] // parts).reshape((-1,) + (1,) * (len(dims) - dim - 1))

    gain = one(*pieces[0])
    for cut in pieces[1:]:
        gain = gain * one(*cut)
    return gain


def noise(key, dims, spread, limit, cuts=(), held_as=jnp.bfloat16):
    drawn = spread * jax.random.normal(key, dims, jnp.float32)
    if cuts:
        drawn = drawn * shard_levels(key, dims, cuts, -0.22, 0.18)
    return jnp.clip(drawn, -limit, limit).astype(held_as)


def setup_inputs(seed: int = 0) -> dict:
    seeds = jax.random.split(jax.random.key(seed), 8)
    return {
        "tokens": noise(seeds[0], (TOKENS, D), 1.0, 6.0, ((0, 32),)),
        "cotangent": noise(seeds[1], (TOKENS, D), 1.0, 6.0, ((0, 32),)),
        "expert_ids": draw_expert_ids(jax.random.fold_in(seeds[7], 71), 0),
        "route_weight": jnp.clip(0.1 + 0.59999999 * jax.random.uniform(seeds[3], (TOKENS, TOP), jnp.float32) ** shard_levels(seeds[3], (TOKENS, TOP), ((0, 32),), -0.2, 0.2), 0.1, 0.7),
        "gate_weight": noise(seeds[4], (EXPERTS, D, FF), D ** -0.5, 0.09375, ((0, 16), (2, 2))),
        "up_weight": noise(seeds[5], (EXPERTS, D, FF), D ** -0.5, 0.09375, ((0, 16), (2, 2))),
        "down_weight": noise(seeds[6], (EXPERTS, FF, D), FF ** -0.5, 0.1875, ((0, 16), (1, 2))),
    }


def rounded(values):
    return lax.optimization_barrier(values.astype(jnp.bfloat16)).astype(jnp.float32)


def reference(tokens, cotangent, expert_ids, route_weight, gate_weight, up_weight, down_weight):
    pair_count = TOKENS * TOP
    slot_total = CAP * DEVICES
    group_size = TOK_DEV * N_EP
    block_width = FF // N_EDP
    flat_ids = expert_ids.reshape(-1)
    flat_weight = route_weight.reshape(-1).astype(jnp.float32)
    owners = (jnp.arange(pair_count, dtype=jnp.int32) // TOP).astype(jnp.int32)
    padded_tokens = jnp.concatenate([tokens, jnp.zeros((1, D), tokens.dtype)], axis=0)
    padded_cotan = jnp.concatenate([cotangent, jnp.zeros((1, D), cotangent.dtype)], axis=0)

    def per_expert(carry, expert):
        out_total, grad_total = carry
        member = flat_ids == expert
        position = (jnp.cumsum(member.astype(jnp.int32)) - 1).astype(jnp.int32)
        target = jnp.where(member, position, slot_total).astype(jnp.int32)
        row_token = jnp.full((slot_total,), TOKENS, jnp.int32).at[target].set(owners, mode="drop")
        row_weight = jnp.zeros((slot_total,), jnp.float32).at[target].set(flat_weight, mode="drop")
        expert_rows = padded_tokens[row_token]
        row_cot = (row_weight[:, None] * padded_cotan[row_token].astype(jnp.float32)).astype(jnp.bfloat16)
        w_gate = gate_weight[expert]
        w_up = up_weight[expert]
        w_down = down_weight[expert]
        gate_act = jnp.dot(expert_rows, w_gate, preferred_element_type=jnp.float32)
        up_act = jnp.dot(expert_rows, w_up, preferred_element_type=jnp.float32)
        sigma_gate = jax.nn.sigmoid(gate_act)
        hidden = (gate_act * sigma_gate * up_act).astype(jnp.bfloat16)
        hidden_blocks = hidden.astype(jnp.float32).reshape(slot_total, N_EDP, block_width)
        down_blocks = w_down.astype(jnp.float32).reshape(N_EDP, block_width, D)
        block_terms = rounded(jnp.einsum("mbf,bfd->bmd", hidden_blocks, down_blocks))
        expert_out = jnp.sum(block_terms, axis=0).astype(jnp.bfloat16)
        out_total = out_total.at[row_token].add(row_weight[:, None] * expert_out.astype(jnp.float32), mode="drop")
        hidden_cot = jnp.dot(row_cot, w_down.T, preferred_element_type=jnp.float32)
        gate_cot = (hidden_cot * up_act * sigma_gate * (1.0 + gate_act * (1.0 - sigma_gate))).astype(jnp.bfloat16)
        up_cot = (hidden_cot * gate_act * sigma_gate).astype(jnp.bfloat16)
        row_group = row_token // group_size

        def group_term(group):
            keep = (row_group == group)[:, None]
            masked = jnp.where(keep, hidden, jnp.zeros_like(hidden))
            return rounded(jnp.dot(masked.T, row_cot, preferred_element_type=jnp.float32))

        group_terms = lax.map(group_term, jnp.arange(N_EDP, dtype=jnp.int32))
        grad_down = jnp.sum(group_terms, axis=0).astype(jnp.bfloat16)
        grad_gate = jnp.dot(expert_rows.T, gate_cot, preferred_element_type=jnp.float32).astype(jnp.bfloat16)
        grad_up = jnp.dot(expert_rows.T, up_cot, preferred_element_type=jnp.float32).astype(jnp.bfloat16)
        gate_cot_blocks = gate_cot.astype(jnp.float32).reshape(slot_total, N_EDP, block_width)
        up_cot_blocks = up_cot.astype(jnp.float32).reshape(slot_total, N_EDP, block_width)
        gate_blocks = w_gate.astype(jnp.float32).reshape(D, N_EDP, block_width)
        up_blocks = w_up.astype(jnp.float32).reshape(D, N_EDP, block_width)
        input_terms = jnp.einsum("mbf,dbf->bmd", gate_cot_blocks, gate_blocks)
        input_terms = input_terms + jnp.einsum("mbf,dbf->bmd", up_cot_blocks, up_blocks)
        row_grad = jnp.sum(rounded(input_terms), axis=0).astype(jnp.bfloat16)
        grad_total = grad_total.at[row_token].add(row_grad.astype(jnp.float32), mode="drop")
        return (out_total, grad_total), (grad_gate, grad_up, grad_down)

    start = (jnp.zeros((TOKENS, D), jnp.float32), jnp.zeros((TOKENS, D), jnp.float32))
    totals, grads = lax.scan(per_expert, start, jnp.arange(EXPERTS, dtype=jnp.int32))
    out_total, grad_total = totals
    grad_gate, grad_up, grad_down = grads
    return (out_total.astype(jnp.bfloat16), grad_total.astype(jnp.bfloat16), grad_gate, grad_up, grad_down)
```

```python
import jax
import jax.numpy as jnp
from jax import lax
from jax.experimental import pallas as pl
from jax.experimental.pallas import tpu as pltpu
from jax.sharding import PartitionSpec as P

F32 = jnp.float32
BF16 = jnp.bfloat16
VMEM_LIMIT = 60 * 1024 * 1024
ROWS_FIRST = (((0,), (0,)), ((), ()))
ROWS_LAST = (((1,), (1,)), ((), ()))
COLS = 512


def matmul(a, b, dims=(((1,), (0,)), ((), ()))):
    return lax.dot_general(a, b, dims, preferred_element_type=F32)


def route_kernel(cap, ids_ref, weight_ref, tok_ref, cot_ref, send_ref, hi_ref, lo_ref, pick_ref, scale_ref):
    tokens, width = hi_ref.shape
    block = 2 * cap

    @pl.when(pl.program_id(0) == 0)
    def _():
        lane = lax.broadcasted_iota(jnp.int32, (tokens, width), 1)
        expert = lane // block
        place = lane % block
        member = jnp.zeros((tokens, width), F32)
        weight = jnp.zeros((tokens, width), F32)
        for k in range(ids_ref.shape[1]):
            hit = ids_ref[:, k : k + 1] == expert
            member = member + jnp.where(hit, 1.0, 0.0)
            weight = weight + jnp.where(hit, weight_ref[:, k : k + 1], 0.0)
        above = lax.broadcasted_iota(jnp.int32, (tokens, tokens), 0) > lax.broadcasted_iota(
            jnp.int32, (tokens, tokens), 1
        )
        rank = matmul(jnp.where(above, 1.0, 0.0).astype(BF16), member.astype(BF16))
        chosen = jnp.where(rank == (place % cap).astype(F32), member, 0.0)
        forward = jnp.where(place < cap, chosen, 0.0)
        backward = chosen - forward
        weighted = forward * weight
        high = weighted.astype(BF16)
        hi_ref[...] = high
        lo_ref[...] = (weighted - high.astype(F32)).astype(BF16)
        pick_ref[...] = backward.astype(BF16)
        scale = jnp.transpose(forward + backward * weight)
        scale_ref[...] = jnp.broadcast_to(jnp.sum(scale, axis=1, keepdims=True), scale_ref.shape)

    first = jnp.where(hi_ref[...] != 0, 1.0, 0.0).astype(BF16)
    rows = matmul(first, tok_ref[...], ROWS_FIRST) + matmul(pick_ref[...], cot_ref[...], ROWS_FIRST)
    send_ref[...] = (rows * scale_ref[:, :1]).astype(BF16)


def route(ids, weight, tokens, cotangent, experts, cap):
    rows, depth = tokens.shape
    width = experts * 2 * cap
    fixed = lambda shape: pl.BlockSpec(shape, lambda j: (0, 0))
    moving = lambda shape: pl.BlockSpec(shape, lambda j: (0, j))
    return pl.pallas_call(
        lambda *refs: route_kernel(cap, *refs),
        grid=(depth // COLS,),
        in_specs=[fixed(ids.shape), fixed(weight.shape), moving((rows, COLS)), moving((rows, COLS))],
        out_specs=[moving((width, COLS)), fixed((rows, width)), fixed((rows, width)), fixed((rows, width))],
        out_shape=[
            jax.ShapeDtypeStruct((width, depth), BF16),
            jax.ShapeDtypeStruct((rows, width), BF16),
            jax.ShapeDtypeStruct((rows, width), BF16),
            jax.ShapeDtypeStruct((rows, width), BF16),
        ],
        scratch_shapes=[pltpu.VMEM((width, 128), F32)],
        compiler_params=pltpu.CompilerParams(vmem_limit_bytes=VMEM_LIMIT),
        name="route",
    )(ids, weight, tokens, cotangent)


def expert_kernel(cap, mine_ref, theirs_ref, gate_ref, up_ref, down_ref, own_ref, other_ref, hid_ref, gate_cot_ref, up_cot_ref):
    half = mine_ref.shape[0]
    total = 2 * half
    depth, hidden_width = gate_ref.shape
    rows = jnp.concatenate([mine_ref[...], theirs_ref[...]], axis=0)
    gate_act = matmul(rows, gate_ref[...])
    up_act = matmul(rows, up_ref[...])
    hidden_cot = matmul(rows, down_ref[...], ROWS_LAST)
    hidden_cot = pltpu.roll(hidden_cot, total - cap, 0)
    place = lax.broadcasted_iota(jnp.int32, (total, hidden_width), 0) % (2 * cap)
    is_token = place < cap
    sigma = jax.nn.sigmoid(gate_act)
    silu = gate_act * sigma
    hidden = jnp.where(is_token, silu * up_act, 0.0)
    gate_cot = jnp.where(is_token, hidden_cot * up_act * sigma * (1.0 + gate_act * (1.0 - sigma)), 0.0)
    up_cot = jnp.where(is_token, hidden_cot * silu, 0.0)
    gate_cot_ref[...] = gate_cot.astype(BF16)
    up_cot_ref[...] = up_cot.astype(BF16)
    hid_ref[...] = pltpu.roll(hidden, cap, 0).astype(BF16)
    hidden = hidden.astype(BF16)
    gate_cot = pltpu.roll(gate_cot, cap, 0).astype(BF16)
    up_cot = pltpu.roll(up_cot, cap, 0).astype(BF16)
    for j in range(depth // COLS):
        cols = pl.ds(j * COLS, COLS)
        back = matmul(hidden, down_ref[:, cols])
        back = back + matmul(gate_cot, gate_ref[cols, :], ROWS_LAST)
        back = back + matmul(up_cot, up_ref[cols, :], ROWS_LAST)
        own_ref[:, cols] = back[:half].astype(BF16)
        other_ref[:, cols] = back[half:].astype(BF16)


def expert(mine, theirs, gate, up, down, cap):
    half, depth = mine.shape
    hidden_width = gate.shape[1]
    whole = pl.BlockSpec(memory_space=pltpu.VMEM)
    return pl.pallas_call(
        lambda *refs: expert_kernel(cap, *refs),
        in_specs=[whole] * 5,
        out_specs=[whole] * 5,
        out_shape=[jax.ShapeDtypeStruct((half, depth), BF16)] * 2
        + [jax.ShapeDtypeStruct((2 * half, hidden_width), BF16)] * 3,
        compiler_params=pltpu.CompilerParams(vmem_limit_bytes=VMEM_LIMIT),
        name="expert",
    )(mine, theirs, gate, up, down)


def grads_kernel(mine_ref, theirs_ref, hid_ref, gate_cot_ref, up_cot_ref, gate_ref, up_ref, down_ref):
    rows = jnp.concatenate([mine_ref[...], theirs_ref[...]], axis=0)
    width = gate_ref.shape[1]
    pair = jnp.concatenate([gate_cot_ref[...], up_cot_ref[...]], axis=1)
    both = matmul(rows, pair, ROWS_FIRST)
    gate_ref[...] = both[:, :width].astype(BF16)
    up_ref[...] = both[:, width:].astype(BF16)
    down_ref[...] = matmul(hid_ref[...], rows, ROWS_FIRST).astype(BF16)


def grads(mine, theirs, hidden, gate_cot, up_cot):
    half, depth = mine.shape
    width = hidden.shape[1]
    fixed = pl.BlockSpec(hidden.shape, lambda j: (0, 0))
    moving = pl.BlockSpec((half, COLS), lambda j: (0, j))
    return pl.pallas_call(
        grads_kernel,
        grid=(depth // COLS,),
        in_specs=[moving, moving, fixed, fixed, fixed],
        out_specs=[
            pl.BlockSpec((COLS, width), lambda j: (j, 0)),
            pl.BlockSpec((COLS, width), lambda j: (j, 0)),
            pl.BlockSpec((width, COLS), lambda j: (0, j)),
        ],
        out_shape=[
            jax.ShapeDtypeStruct((depth, width), BF16),
            jax.ShapeDtypeStruct((depth, width), BF16),
            jax.ShapeDtypeStruct((width, depth), BF16),
        ],
        compiler_params=pltpu.CompilerParams(vmem_limit_bytes=VMEM_LIMIT),
        name="weight_grads",
    )(mine, theirs, hidden, gate_cot, up_cot)


def combine_kernel(back_ref, hi_ref, lo_ref, pick_ref, out_ref, grad_ref):
    back = back_ref[...]
    out_ref[...] = (matmul(hi_ref[...], back) + matmul(lo_ref[...], back)).astype(BF16)
    grad_ref[...] = matmul(pick_ref[...], back).astype(BF16)


def combine(back, high, low, pick):
    width, depth = back.shape
    rows = high.shape[0]
    fixed = pl.BlockSpec((rows, width), lambda j: (0, 0))
    moving = pl.BlockSpec((rows, COLS), lambda j: (0, j))
    return pl.pallas_call(
        combine_kernel,
        grid=(depth // COLS,),
        in_specs=[pl.BlockSpec((width, COLS), lambda j: (0, j)), fixed, fixed, fixed],
        out_specs=[moving, moving],
        out_shape=[jax.ShapeDtypeStruct((rows, depth), BF16)] * 2,
        compiler_params=pltpu.CompilerParams(vmem_limit_bytes=VMEM_LIMIT),
        name="combine",
    )(back, high, low, pick)


def per_device(tokens, cotangent, expert_ids, route_weight, gate_weight, up_weight, down_weight):
    experts = lax.axis_size("ep")
    cap = tokens.shape[0] // 32
    depth = tokens.shape[1]
    swap = [(0, 1), (1, 0)]
    send, high, low, pick = route(expert_ids, route_weight, tokens, cotangent, experts, cap)

    def exchange(rows):
        blocks = rows.reshape(experts, 2 * cap, depth)
        return lax.all_to_all(blocks, "ep", split_axis=0, concat_axis=0, tiled=True).reshape(rows.shape)

    mine = exchange(send)
    theirs = lax.ppermute(mine, "edp", swap)
    own, other, hidden, gate_cot, up_cot = expert(
        mine, theirs, gate_weight[0], up_weight[0], down_weight[0], cap
    )
    arrived = lax.ppermute(other, "edp", swap)
    total = (own.astype(F32) + arrived.astype(F32)).astype(BF16)
    back = exchange(total)
    grad_gate, grad_up, grad_down = grads(mine, theirs, hidden, gate_cot, up_cot)
    routed_out, token_grad = combine(back, high, low, pick)
    return (routed_out, token_grad, grad_gate[None], grad_up[None], grad_down[None])


def solution(mesh):
    in_specs = (
        P(("edp", "ep"), None),
        P(("edp", "ep"), None),
        P(("edp", "ep"), None),
        P(("edp", "ep"), None),
        P("ep", None, "edp"),
        P("ep", None, "edp"),
        P("ep", "edp", None),
    )
    out_specs = (
        P(("edp", "ep"), None),
        P(("edp", "ep"), None),
        P("ep", None, "edp"),
        P("ep", None, "edp"),
        P("ep", "edp", None),
    )
    return jax.shard_map(
        per_device, mesh=mesh, in_specs=in_specs, out_specs=out_specs, check_vma=False
    )
```

```python
import jax
import jax.numpy as jnp
from jax import lax
from jax.experimental import pallas as pl
from jax.experimental.pallas import tpu as pltpu
from jax.sharding import PartitionSpec as P

F32 = jnp.float32
BF16 = jnp.bfloat16
MIB = 1024 * 1024
SCOPED = 16 * MIB
ROWS_FIRST = (((0,), (0,)), ((), ()))
ROWS_LAST = (((1,), (1,)), ((), ()))
COLS = 512


def matmul(a, b, dims=(((1,), (0,)), ((), ()))):
    return lax.dot_general(a, b, dims, preferred_element_type=F32)


WHOLE = pl.BlockSpec(memory_space=pltpu.VMEM)
REMOTE = pl.BlockSpec(memory_space=pl.ANY)


def spread(depth):
    return [pl.ds(j * COLS, COLS) for j in range(depth // COLS)]


def in_hbm(*arrays):
    return [pltpu.with_memory_space_constraint(a, pltpu.HBM) for a in arrays]


def in_vmem(*arrays):
    return [pltpu.with_memory_space_constraint(a, pltpu.VMEM) for a in arrays]


def route_kernel(
    cap, ids_hbm, weight_hbm, tok_hbm, cot_hbm, send_ref, select_hbm,
    ids_ref, weight_ref, tok_ref, cot_ref, select_ref, small_sems, sems,
):
    width, tokens = send_ref.shape[0], tok_ref.shape[0]
    block = 2 * cap
    parts = spread(tok_hbm.shape[1])
    small = [
        pltpu.make_async_copy(ids_hbm, ids_ref, small_sems.at[0]),
        pltpu.make_async_copy(weight_hbm, weight_ref, small_sems.at[1]),
    ]
    copies = [
        (
            pltpu.make_async_copy(tok_hbm.at[:, cols], tok_ref.at[:, cols], sems.at[0, j]),
            pltpu.make_async_copy(cot_hbm.at[:, cols], cot_ref.at[:, cols], sems.at[1, j]),
        )
        for j, cols in enumerate(parts)
    ]
    for copy in small:
        copy.start()
    for pair in copies:
        for copy in pair:
            copy.start()
    slot = lax.broadcasted_iota(jnp.int32, (width, tokens), 0)
    expert = slot // block
    place = slot % block
    before = lax.broadcasted_iota(jnp.int32, (tokens, tokens), 0) < lax.broadcasted_iota(
        jnp.int32, (tokens, tokens), 1
    )
    before = jnp.where(before, 1.0, 0.0).astype(BF16)
    for copy in small:
        copy.wait()
    member = jnp.zeros((width, tokens), F32)
    weight = jnp.zeros((width, tokens), F32)
    for k in range(ids_ref.shape[0]):
        hit = ids_ref[k : k + 1, :] == expert
        member = member + jnp.where(hit, 1.0, 0.0)
        weight = weight + jnp.where(hit, weight_ref[k : k + 1, :], 0.0)
    rank = matmul(member.astype(BF16), before)
    chosen = jnp.where(rank == (place % cap).astype(F32), member, 0.0)
    forward = jnp.where(place < cap, chosen, 0.0)
    backward = chosen - forward
    scale = jnp.sum(forward + backward * weight, axis=1, keepdims=True)
    first = forward.astype(BF16)
    second = backward.astype(BF16)
    for pair, cols in zip(copies, parts):
        for copy in pair:
            copy.wait()
        rows = matmul(first, tok_ref[:, cols]) + matmul(second, cot_ref[:, cols])
        send_ref[:, cols] = (rows * scale).astype(BF16)
    weighted = jnp.transpose(forward * weight)
    high = weighted.astype(BF16)
    select_ref[0] = high
    select_ref[1] = (weighted - high.astype(F32)).astype(BF16)
    select_ref[2] = jnp.transpose(backward).astype(BF16)
    copy = pltpu.make_async_copy(select_ref, select_hbm, small_sems.at[2])
    copy.start()
    copy.wait()


def route(ids, weight, tokens, cotangent, experts, cap):
    rows, depth = tokens.shape
    width = experts * 2 * cap
    return pl.pallas_call(
        lambda *refs: route_kernel(cap, *refs),
        in_specs=[REMOTE] * 4,
        out_specs=[WHOLE, REMOTE],
        out_shape=[pltpu.VMEM((width, depth), BF16), pltpu.HBM((3, rows, width), BF16)],
        scratch_shapes=[
            pltpu.VMEM(ids.shape, jnp.int32),
            pltpu.VMEM(weight.shape, F32),
            pltpu.VMEM((rows, depth), BF16),
            pltpu.VMEM((rows, depth), BF16),
            pltpu.VMEM((3, rows, width), BF16),
            pltpu.SemaphoreType.DMA((3,)),
            pltpu.SemaphoreType.DMA((2, depth // COLS)),
        ],
        compiler_params=pltpu.CompilerParams(vmem_limit_bytes=8 * MIB),
        name="route",
    )(*in_hbm(ids, weight, tokens, cotangent))


def load_kernel(after_ref, *refs):
    sems = refs[-1]
    count = (len(refs) - 1) // 2
    copies = [pltpu.make_async_copy(refs[i], refs[count + i], sems.at[i]) for i in range(count)]
    for copy in copies:
        copy.start()
    for copy in copies:
        copy.wait()


def load(after, arrays):
    return pl.pallas_call(
        load_kernel,
        in_specs=[REMOTE] * (1 + len(arrays)),
        out_specs=[WHOLE] * len(arrays),
        out_shape=[pltpu.VMEM(a.shape, a.dtype) for a in arrays],
        scratch_shapes=[pltpu.SemaphoreType.DMA((len(arrays),))],
        compiler_params=pltpu.CompilerParams(vmem_limit_bytes=2 * MIB),
        name="load_weights",
    )(after, *in_hbm(*arrays))


def back_rows(hidden, gate_cot, up_cot, gate_ref, up_ref, down_ref, own_ref, other_ref, first, count):
    half = own_ref.shape[0]
    for j in range(count):
        cols = pl.ds((first + j) * COLS, COLS)
        back = matmul(hidden, down_ref[:, cols])
        back = back + matmul(gate_cot, gate_ref[cols, :], ROWS_LAST)
        back = back + matmul(up_cot, up_ref[cols, :], ROWS_LAST)
        here = pl.ds(j * COLS, COLS)
        own_ref[:, here] = back[:half].astype(BF16)
        other_ref[:, here] = back[half:].astype(BF16)


def expert_kernel(
    cap, mine_ref, theirs_ref, gate_ref, up_hbm, down_hbm,
    own_ref, other_ref, hid_ref, gate_cot_ref, up_cot_ref, stack_ref, up_ref, down_ref, sems,
):
    half = mine_ref.shape[0]
    total = 2 * half
    depth, hidden_width = gate_ref.shape
    load_up = pltpu.make_async_copy(up_hbm, up_ref, sems.at[0])
    load_down = pltpu.make_async_copy(down_hbm, down_ref, sems.at[1])
    load_up.start()
    load_down.start()
    rows = jnp.concatenate([mine_ref[...], theirs_ref[...]], axis=0)
    gate_act = matmul(rows, gate_ref[...])
    load_up.wait()
    up_act = matmul(rows, up_ref[...])
    load_down.wait()
    hidden_cot = matmul(rows, down_ref[...], ROWS_LAST)
    hidden_cot = pltpu.roll(hidden_cot, total - cap, 0)
    place = lax.broadcasted_iota(jnp.int32, (total, hidden_width), 0) % (2 * cap)
    is_token = place < cap
    sigma = jax.nn.sigmoid(gate_act)
    silu = gate_act * sigma
    hidden = jnp.where(is_token, silu * up_act, 0.0)
    gate_cot = jnp.where(is_token, hidden_cot * up_act * sigma * (1.0 + gate_act * (1.0 - sigma)), 0.0)
    up_cot = jnp.where(is_token, hidden_cot * silu, 0.0)
    gate_cot_ref[...] = gate_cot.astype(BF16)
    up_cot_ref[...] = up_cot.astype(BF16)
    hid_ref[...] = pltpu.roll(hidden, cap, 0).astype(BF16)
    stack_ref[0] = hidden.astype(BF16)
    stack_ref[1] = pltpu.roll(gate_cot, cap, 0).astype(BF16)
    stack_ref[2] = pltpu.roll(up_cot, cap, 0).astype(BF16)
    back_rows(
        stack_ref[0], stack_ref[1], stack_ref[2], gate_ref, up_ref, down_ref, own_ref, other_ref,
        0, own_ref.shape[1] // COLS,
    )


def expert(mine, theirs, gate, up, down, cap):
    half, depth = mine.shape
    hidden_width = gate.shape[1]
    early = early_cols(depth)
    return pl.pallas_call(
        lambda *refs: expert_kernel(cap, *refs),
        in_specs=[WHOLE] * 3 + [REMOTE] * 2,
        out_specs=[WHOLE] * 8,
        out_shape=[pltpu.VMEM((half, early), BF16)] * 2
        + [pltpu.VMEM((2 * half, hidden_width), BF16)] * 3
        + [pltpu.VMEM((3, 2 * half, hidden_width), BF16), pltpu.VMEM(up.shape, BF16), pltpu.VMEM(down.shape, BF16)],
        scratch_shapes=[pltpu.SemaphoreType.DMA((2,))],
        compiler_params=pltpu.CompilerParams(vmem_limit_bytes=SCOPED),
        name="expert",
    )(*in_vmem(mine, theirs, gate), *in_hbm(up, down))


def early_cols(depth):
    return depth // COLS // 2 * COLS


def late_kernel(stack_ref, gate_ref, up_ref, down_ref, own_ref, other_ref):
    count = own_ref.shape[1] // COLS
    first = gate_ref.shape[0] // COLS - count
    back_rows(
        stack_ref[0], stack_ref[1], stack_ref[2], gate_ref, up_ref, down_ref, own_ref, other_ref, first, count
    )


def late_rows(stack, gate, up, down):
    half = stack.shape[1] // 2
    depth = gate.shape[0]
    late = depth - early_cols(depth)
    return pl.pallas_call(
        late_kernel,
        in_specs=[WHOLE] * 4,
        out_specs=[WHOLE] * 2,
        out_shape=[pltpu.VMEM((half, late), BF16)] * 2,
        compiler_params=pltpu.CompilerParams(vmem_limit_bytes=8 * MIB),
        name="late_rows",
    )(*in_vmem(stack, gate, up, down))


def add_kernel(own_early, other_early, own_late, other_late, out_hbm, out_ref, sems):
    early = own_early.shape[1]
    copies = []
    for j, cols in enumerate(spread(out_ref.shape[1])):
        if j * COLS < early:
            a, b, here = own_early, other_early, pl.ds(j * COLS, COLS)
        else:
            a, b, here = own_late, other_late, pl.ds(j * COLS - early, COLS)
        out_ref[:, cols] = (a[:, here].astype(F32) + b[:, here].astype(F32)).astype(BF16)
        copy = pltpu.make_async_copy(out_ref.at[:, cols], out_hbm.at[:, cols], sems.at[j])
        copy.start()
        copies.append(copy)
    for copy in copies:
        copy.wait()


def add_rows(own_early, other_early, own_late, other_late):
    rows = own_early.shape[0]
    depth = own_early.shape[1] + own_late.shape[1]
    return pl.pallas_call(
        add_kernel,
        in_specs=[WHOLE] * 4,
        out_specs=REMOTE,
        out_shape=pltpu.HBM((rows, depth), BF16),
        scratch_shapes=[pltpu.VMEM((rows, depth), BF16), pltpu.SemaphoreType.DMA((depth // COLS,))],
        compiler_params=pltpu.CompilerParams(vmem_limit_bytes=8 * MIB),
        name="add_rows",
    )(*in_vmem(own_early, other_early, own_late, other_late))


def grads_kernel(mine_ref, theirs_ref, hid_ref, gate_cot_ref, up_cot_ref, gate_ref, up_ref, down_ref):
    cols = pl.ds(pl.multiple_of(pl.program_id(0) * COLS, COLS), COLS)
    rows = jnp.concatenate([mine_ref[:, cols], theirs_ref[:, cols]], axis=0)
    width = gate_ref.shape[1]
    pair = jnp.concatenate([gate_cot_ref[...], up_cot_ref[...]], axis=1)
    both = matmul(rows, pair, ROWS_FIRST)
    gate_ref[...] = both[:, :width].astype(BF16)
    up_ref[...] = both[:, width:].astype(BF16)
    down_ref[...] = matmul(hid_ref[...], rows, ROWS_FIRST).astype(BF16)


def grads(mine, theirs, hidden, gate_cot, up_cot):
    half, depth = mine.shape
    width = hidden.shape[1]
    return pl.pallas_call(
        grads_kernel,
        grid=(depth // COLS,),
        in_specs=[WHOLE] * 5,
        out_specs=[
            pl.BlockSpec((COLS, width), lambda j: (j, 0)),
            pl.BlockSpec((COLS, width), lambda j: (j, 0)),
            pl.BlockSpec((width, COLS), lambda j: (0, j)),
        ],
        out_shape=[
            jax.ShapeDtypeStruct((depth, width), BF16),
            jax.ShapeDtypeStruct((depth, width), BF16),
            jax.ShapeDtypeStruct((width, depth), BF16),
        ],
        compiler_params=pltpu.CompilerParams(vmem_limit_bytes=SCOPED),
        name="weight_grads",
    )(*in_vmem(mine, theirs, hidden, gate_cot, up_cot))


def combine_kernel(back_ref, select_hbm, out_hbm, grad_hbm, select_ref, out_ref, grad_ref, select_sem, sems):
    load_select = pltpu.make_async_copy(select_hbm, select_ref, select_sem)
    load_select.start()
    load_select.wait()
    copies = []
    for j, cols in enumerate(spread(back_ref.shape[1])):
        back = back_ref[:, cols]
        out_ref[:, cols] = (matmul(select_ref[0], back) + matmul(select_ref[1], back)).astype(BF16)
        copy = pltpu.make_async_copy(out_ref.at[:, cols], out_hbm.at[:, cols], sems.at[0, j])
        copy.start()
        copies.append(copy)
        grad_ref[:, cols] = matmul(select_ref[2], back).astype(BF16)
        copy = pltpu.make_async_copy(grad_ref.at[:, cols], grad_hbm.at[:, cols], sems.at[1, j])
        copy.start()
        copies.append(copy)
    for copy in copies:
        copy.wait()


def combine(back, select):
    width, depth = back.shape
    rows = select.shape[1]
    return pl.pallas_call(
        combine_kernel,
        in_specs=[WHOLE, REMOTE],
        out_specs=[REMOTE, REMOTE],
        out_shape=[pltpu.HBM((rows, depth), BF16)] * 2,
        scratch_shapes=[
            pltpu.VMEM(select.shape, BF16),
            pltpu.VMEM((rows, depth), BF16),
            pltpu.VMEM((rows, depth), BF16),
            pltpu.SemaphoreType.DMA,
            pltpu.SemaphoreType.DMA((2, depth // COLS)),
        ],
        compiler_params=pltpu.CompilerParams(vmem_limit_bytes=8 * MIB),
        name="combine",
    )(*in_vmem(back), *in_hbm(select))


def per_device(tokens, cotangent, expert_ids, route_weight, gate_weight, up_weight, down_weight):
    experts = lax.axis_size("ep")
    cap = tokens.shape[0] // 32
    depth = tokens.shape[1]
    swap = [(0, 1), (1, 0)]
    send, select = route(expert_ids.T, route_weight.T, tokens, cotangent, experts, cap)

    def exchange(rows):
        blocks = rows.reshape(experts, 2 * cap, depth)
        return lax.all_to_all(blocks, "ep", split_axis=0, concat_axis=0, tiled=True).reshape(rows.shape)

    mine = exchange(send)
    theirs = lax.ppermute(mine, "edp", swap)
    (gate,) = load(mine, [gate_weight[0]])
    own_early, other_early, hidden, gate_cot, up_cot, stack, up, down = expert(
        mine, theirs, gate, up_weight[0], down_weight[0], cap
    )
    arrived_early = lax.ppermute(other_early, "edp", swap)
    own_late, other_late = late_rows(stack, gate, up, down)
    other_late, arrived_early = lax.optimization_barrier((other_late, arrived_early))
    arrived_late = lax.ppermute(other_late, "edp", swap)
    back = exchange(add_rows(own_early, arrived_early, own_late, arrived_late))
    grad_gate, grad_up, grad_down = grads(mine, theirs, hidden, gate_cot, up_cot)
    routed_out, token_grad = combine(back, select)
    return (routed_out, token_grad, grad_gate[None], grad_up[None], grad_down[None])


def solution(mesh):
    in_specs = (
        P(("edp", "ep"), None),
        P(("edp", "ep"), None),
        P(("edp", "ep"), None),
        P(("edp", "ep"), None),
        P("ep", None, "edp"),
        P("ep", None, "edp"),
        P("ep", "edp", None),
    )
    out_specs = (
        P(("edp", "ep"), None),
        P(("edp", "ep"), None),
        P("ep", None, "edp"),
        P("ep", None, "edp"),
        P("ep", "edp", None),
    )
    return jax.shard_map(
        per_device, mesh=mesh, in_specs=in_specs, out_specs=out_specs, check_vma=False
    )
```

```python
import jax
import jax.numpy as jnp
from jax import lax
from jax.experimental import pallas as pl
from jax.experimental.pallas import tpu as pltpu
from jax.sharding import PartitionSpec as P

F32 = jnp.float32
BF16 = jnp.bfloat16
MIB = 1024 * 1024
SCOPED = 16 * MIB
ROWS_FIRST = (((0,), (0,)), ((), ()))
ROWS_LAST = (((1,), (1,)), ((), ()))
COLS = 512


def matmul(a, b, dims=(((1,), (0,)), ((), ()))):
    return lax.dot_general(a, b, dims, preferred_element_type=F32)


WHOLE = pl.BlockSpec(memory_space=pltpu.VMEM)
REMOTE = pl.BlockSpec(memory_space=pl.ANY)


def spread(depth):
    return [pl.ds(j * COLS, COLS) for j in range(depth // COLS)]


def in_hbm(*arrays):
    return [pltpu.with_memory_space_constraint(a, pltpu.HBM) for a in arrays]


def in_vmem(*arrays):
    return [pltpu.with_memory_space_constraint(a, pltpu.VMEM) for a in arrays]


def slots(cap, width, ids_ref, weight_ref, waits):
    tokens = ids_ref.shape[1]
    slot = lax.broadcasted_iota(jnp.int32, (width, tokens), 0)
    expert = slot // (2 * cap)
    place = slot % (2 * cap)
    before = lax.broadcasted_iota(jnp.int32, (tokens, tokens), 0) < lax.broadcasted_iota(
        jnp.int32, (tokens, tokens), 1
    )
    before = jnp.where(before, 1.0, 0.0).astype(BF16)
    for copy in waits:
        copy.wait()
    member = jnp.zeros((width, tokens), F32)
    weight = jnp.zeros((width, tokens), F32)
    for k in range(ids_ref.shape[0]):
        hit = ids_ref[k : k + 1, :] == expert
        member = jnp.where(hit, 1.0, member)
        weight = jnp.where(hit, weight_ref[k : k + 1, :], weight)
    rank = matmul(member.astype(BF16), before)
    chosen = jnp.where(rank == (place % cap).astype(F32), member, 0.0)
    forward = jnp.where(place < cap, chosen, 0.0)
    return forward, chosen - forward, weight


def route_kernel(
    cap, ids_hbm, weight_hbm, tok_hbm, cot_hbm, send_ref, ids_ref, weight_ref, tok_ref, cot_ref, small_sems, sems
):
    parts = spread(tok_hbm.shape[1])
    small = [
        pltpu.make_async_copy(ids_hbm, ids_ref, small_sems.at[0]),
        pltpu.make_async_copy(weight_hbm, weight_ref, small_sems.at[1]),
    ]
    copies = [
        (
            pltpu.make_async_copy(tok_hbm.at[:, cols], tok_ref.at[:, cols], sems.at[0, j]),
            pltpu.make_async_copy(cot_hbm.at[:, cols], cot_ref.at[:, cols], sems.at[1, j]),
        )
        for j, cols in enumerate(parts)
    ]
    for copy in small:
        copy.start()
    for pair in copies:
        for copy in pair:
            copy.start()
    forward, backward, weight = slots(cap, send_ref.shape[0], ids_ref, weight_ref, small)
    scale = jnp.sum(forward + backward * weight, axis=1, keepdims=True)
    picks = jnp.concatenate([forward, backward], axis=1).astype(BF16)
    for pair, cols in zip(copies, parts):
        for copy in pair:
            copy.wait()
        rows = matmul(picks, jnp.concatenate([tok_ref[:, cols], cot_ref[:, cols]], axis=0))
        send_ref[:, cols] = (rows * scale).astype(BF16)


def route(ids, weight, tokens, cotangent, experts, cap):
    rows, depth = tokens.shape
    width = experts * 2 * cap
    return pl.pallas_call(
        lambda *refs: route_kernel(cap, *refs),
        in_specs=[REMOTE] * 4,
        out_specs=WHOLE,
        out_shape=pltpu.VMEM((width, depth), BF16),
        scratch_shapes=[
            pltpu.VMEM(ids.shape, jnp.int32),
            pltpu.VMEM(weight.shape, F32),
            pltpu.VMEM((rows, depth), BF16),
            pltpu.VMEM((rows, depth), BF16),
            pltpu.SemaphoreType.DMA((2,)),
            pltpu.SemaphoreType.DMA((2, depth // COLS)),
        ],
        compiler_params=pltpu.CompilerParams(vmem_limit_bytes=16 * MIB),
        name="route",
    )(*in_hbm(ids, weight, tokens, cotangent))


def select_kernel(cap, ids_hbm, weight_hbm, select_hbm, ids_ref, weight_ref, select_ref, sems):
    small = [
        pltpu.make_async_copy(ids_hbm, ids_ref, sems.at[0]),
        pltpu.make_async_copy(weight_hbm, weight_ref, sems.at[1]),
    ]
    for copy in small:
        copy.start()
    forward, backward, weight = slots(cap, select_ref.shape[1], ids_ref, weight_ref, small)
    weighted = jnp.transpose(forward * weight)
    high = weighted.astype(BF16)
    count = high.shape[0]
    select_ref[:count] = high
    select_ref[count : 2 * count] = (weighted - high.astype(F32)).astype(BF16)
    select_ref[2 * count :] = jnp.transpose(backward).astype(BF16)
    copy = pltpu.make_async_copy(select_ref, select_hbm, sems.at[2])
    copy.start()
    copy.wait()


def selectors(ids, weight, experts, cap):
    shape = (3 * ids.shape[1], experts * 2 * cap)
    return pl.pallas_call(
        lambda *refs: select_kernel(cap, *refs),
        in_specs=[REMOTE] * 2,
        out_specs=REMOTE,
        out_shape=pltpu.HBM(shape, BF16),
        scratch_shapes=[
            pltpu.VMEM(ids.shape, jnp.int32),
            pltpu.VMEM(weight.shape, F32),
            pltpu.VMEM(shape, BF16),
            pltpu.SemaphoreType.DMA((3,)),
        ],
        compiler_params=pltpu.CompilerParams(vmem_limit_bytes=8 * MIB),
        name="selectors",
    )(*in_hbm(ids, weight))


def compact_kernel(cap, rows_ref, tok_ref, cot_ref):
    groups = rows_ref.shape[0] // (2 * cap)
    half = tok_ref.shape[0]
    for cols in spread(rows_ref.shape[1]):
        both = rows_ref[:, cols].astype(F32).reshape(groups, 2, cap, COLS)
        tok_ref[:, cols] = both[:, 0].reshape(half, COLS).astype(BF16)
        cot_ref[:, cols] = both[:, 1].reshape(half, COLS).astype(BF16)


def compact(rows, cap):
    half, depth = rows.shape[0] // 2, rows.shape[1]
    return pl.pallas_call(
        lambda *refs: compact_kernel(cap, *refs),
        in_specs=[WHOLE],
        out_specs=[WHOLE] * 2,
        out_shape=[pltpu.VMEM((half, depth), BF16)] * 2,
        compiler_params=pltpu.CompilerParams(vmem_limit_bytes=8 * MIB),
        name="compact",
    )(*in_vmem(rows))


def split_store(value, own_ref, other_ref, cols):
    half = own_ref.shape[0]
    own_ref[:, cols] = value[:half].astype(BF16)
    other_ref[:, cols] = value[half:].astype(BF16)


def forward_kernel(
    mine_ref, theirs_ref, gate_ref, up_ref, down_ref, own_ref, other_ref, hid_ref, gate_act_ref, up_act_ref
):
    rows = jnp.concatenate([mine_ref[...], theirs_ref[...]], axis=0)
    gate_act = matmul(rows, gate_ref[...])
    up_act = matmul(rows, up_ref[...])
    gate_act_ref[...] = gate_act
    up_act_ref[...] = up_act
    hidden = (gate_act * jax.nn.sigmoid(gate_act) * up_act).astype(BF16)
    hid_ref[...] = hidden
    for cols in spread(mine_ref.shape[1]):
        split_store(matmul(hidden, down_ref[:, cols]), own_ref, other_ref, cols)


def forward(mine, theirs, gate, up, down):
    half, depth = mine.shape
    width = gate.shape[1]
    return pl.pallas_call(
        forward_kernel,
        in_specs=[WHOLE] * 5,
        out_specs=[WHOLE] * 5,
        out_shape=[
            pltpu.VMEM((half, depth), BF16),
            pltpu.VMEM((half, depth), BF16),
            pltpu.VMEM((2 * half, width), BF16),
            pltpu.VMEM((2 * half, width), F32),
            pltpu.VMEM((2 * half, width), F32),
        ],
        compiler_params=pltpu.CompilerParams(vmem_limit_bytes=SCOPED),
        name="expert_forward",
    )(*in_vmem(mine, theirs, gate, up, down))


def row_grads(gate_cot, up_cot, gate_ref, up_ref, own_ref, other_ref, first):
    for j in range(own_ref.shape[1] // COLS):
        cols = pl.ds((first + j) * COLS, COLS)
        back = matmul(gate_cot, gate_ref[cols, :], ROWS_LAST)
        back = back + matmul(up_cot, up_ref[cols, :], ROWS_LAST)
        split_store(back, own_ref, other_ref, pl.ds(j * COLS, COLS))


def backward_kernel(
    mine_ref, theirs_ref, gate_ref, up_ref, down_ref, gate_act_ref, up_act_ref,
    own_ref, other_ref, gate_cot_ref, up_cot_ref,
):
    rows = jnp.concatenate([mine_ref[...], theirs_ref[...]], axis=0)
    hidden_cot = matmul(rows, down_ref[...], ROWS_LAST)
    gate_act = gate_act_ref[...]
    sigma = jax.nn.sigmoid(gate_act)
    gate_cot = (hidden_cot * up_act_ref[...] * sigma * (1.0 + gate_act * (1.0 - sigma))).astype(BF16)
    up_cot = (hidden_cot * (gate_act * sigma)).astype(BF16)
    gate_cot_ref[...] = gate_cot
    up_cot_ref[...] = up_cot
    row_grads(gate_cot, up_cot, gate_ref, up_ref, own_ref, other_ref, 0)


def early_cols(depth):
    return depth // COLS * 4 // 7 * COLS


def backward(mine, theirs, gate, up, down, gate_act, up_act):
    half, depth = mine.shape
    width = gate.shape[1]
    early = early_cols(depth)
    return pl.pallas_call(
        backward_kernel,
        in_specs=[WHOLE] * 7,
        out_specs=[WHOLE] * 4,
        out_shape=[pltpu.VMEM((half, early), BF16)] * 2 + [pltpu.VMEM((2 * half, width), BF16)] * 2,
        compiler_params=pltpu.CompilerParams(vmem_limit_bytes=SCOPED),
        name="expert_backward",
    )(*in_vmem(mine, theirs, gate, up, down, gate_act, up_act))


def late_kernel(gate_cot_ref, up_cot_ref, gate_ref, up_ref, own_ref, other_ref):
    first = (gate_ref.shape[0] - own_ref.shape[1]) // COLS
    row_grads(gate_cot_ref[...], up_cot_ref[...], gate_ref, up_ref, own_ref, other_ref, first)


def late_rows(gate_cot, up_cot, gate, up):
    half = gate_cot.shape[0] // 2
    depth = gate.shape[0]
    late = depth - early_cols(depth)
    return pl.pallas_call(
        late_kernel,
        in_specs=[WHOLE] * 4,
        out_specs=[WHOLE] * 2,
        out_shape=[pltpu.VMEM((half, late), BF16)] * 2,
        compiler_params=pltpu.CompilerParams(vmem_limit_bytes=8 * MIB),
        name="late_rows",
    )(*in_vmem(gate_cot, up_cot, gate, up))


def add_kernel(cap, *refs):
    own_out, arrived_out, own_early, arrived_early, own_late, arrived_late, out_hbm, out_ref, sems = refs
    early = own_early.shape[1]
    rows = out_ref.shape[0]
    groups = rows // (2 * cap)
    copies = []
    for j, cols in enumerate(spread(out_ref.shape[1])):
        if j * COLS < early:
            a, b, here = own_early, arrived_early, pl.ds(j * COLS, COLS)
        else:
            a, b, here = own_late, arrived_late, pl.ds(j * COLS - early, COLS)
        out = own_out[:, cols].astype(F32) + arrived_out[:, cols].astype(F32)
        grad = a[:, here].astype(F32) + b[:, here].astype(F32)
        both = jnp.concatenate([out.reshape(groups, cap, COLS), grad.reshape(groups, cap, COLS)], axis=1)
        out_ref[:, cols] = both.reshape(rows, COLS).astype(BF16)
        copy = pltpu.make_async_copy(out_ref.at[:, cols], out_hbm.at[:, cols], sems.at[j])
        copy.start()
        copies.append(copy)
    for copy in copies:
        copy.wait()


def add_rows(cap, *arrays):
    half, depth = arrays[0].shape
    return pl.pallas_call(
        lambda *refs: add_kernel(cap, *refs),
        in_specs=[WHOLE] * 6,
        out_specs=REMOTE,
        out_shape=pltpu.HBM((2 * half, depth), BF16),
        scratch_shapes=[pltpu.VMEM((2 * half, depth), BF16), pltpu.SemaphoreType.DMA((depth // COLS,))],
        compiler_params=pltpu.CompilerParams(vmem_limit_bytes=16 * MIB),
        name="add_rows",
    )(*in_vmem(*arrays))


def grads_kernel(
    tok_mine, tok_theirs, cot_mine, cot_theirs, hid_ref, gate_cot_ref, up_cot_ref, gate_ref, up_ref, down_ref
):
    cols = pl.ds(pl.multiple_of(pl.program_id(0) * COLS, COLS), COLS)
    width = gate_ref.shape[1]
    pair = jnp.concatenate([gate_cot_ref[...], up_cot_ref[...]], axis=1)
    tokens = jnp.concatenate([tok_mine[:, cols], tok_theirs[:, cols]], axis=0)
    both = matmul(tokens, pair, ROWS_FIRST)
    gate_ref[...] = both[:, :width].astype(BF16)
    up_ref[...] = both[:, width:].astype(BF16)
    cotangent = jnp.concatenate([cot_mine[:, cols], cot_theirs[:, cols]], axis=0)
    down_ref[...] = matmul(hid_ref[...], cotangent, ROWS_FIRST).astype(BF16)


def grads(tok_mine, tok_theirs, cot_mine, cot_theirs, hidden, gate_cot, up_cot):
    depth = tok_mine.shape[1]
    width = hidden.shape[1]
    return pl.pallas_call(
        grads_kernel,
        grid=(depth // COLS,),
        in_specs=[WHOLE] * 7,
        out_specs=[
            pl.BlockSpec((COLS, width), lambda j: (j, 0)),
            pl.BlockSpec((COLS, width), lambda j: (j, 0)),
            pl.BlockSpec((width, COLS), lambda j: (0, j)),
        ],
        out_shape=[
            jax.ShapeDtypeStruct((depth, width), BF16),
            jax.ShapeDtypeStruct((depth, width), BF16),
            jax.ShapeDtypeStruct((width, depth), BF16),
        ],
        compiler_params=pltpu.CompilerParams(vmem_limit_bytes=SCOPED),
        name="weight_grads",
    )(*in_vmem(tok_mine, tok_theirs, cot_mine, cot_theirs, hidden, gate_cot, up_cot))


def combine_kernel(back_ref, select_hbm, out_hbm, grad_hbm, select_ref, out_ref, grad_ref, select_sem, sems):
    load_select = pltpu.make_async_copy(select_hbm, select_ref, select_sem)
    load_select.start()
    load_select.wait()
    count = out_ref.shape[0]
    copies = []
    for j, cols in enumerate(spread(back_ref.shape[1])):
        sums = matmul(select_ref[...], back_ref[:, cols])
        out_ref[:, cols] = (sums[:count] + sums[count : 2 * count]).astype(BF16)
        grad_ref[:, cols] = sums[2 * count :].astype(BF16)
        pair = [
            pltpu.make_async_copy(out_ref.at[:, cols], out_hbm.at[:, cols], sems.at[0, j]),
            pltpu.make_async_copy(grad_ref.at[:, cols], grad_hbm.at[:, cols], sems.at[1, j]),
        ]
        for copy in pair:
            copy.start()
        copies.extend(pair)
    for copy in copies:
        copy.wait()


def combine(back, select):
    width, depth = back.shape
    rows = select.shape[0] // 3
    return pl.pallas_call(
        combine_kernel,
        in_specs=[WHOLE, REMOTE],
        out_specs=[REMOTE, REMOTE],
        out_shape=[pltpu.HBM((rows, depth), BF16)] * 2,
        scratch_shapes=[
            pltpu.VMEM(select.shape, BF16),
            pltpu.VMEM((rows, depth), BF16),
            pltpu.VMEM((rows, depth), BF16),
            pltpu.SemaphoreType.DMA,
            pltpu.SemaphoreType.DMA((2, depth // COLS)),
        ],
        compiler_params=pltpu.CompilerParams(vmem_limit_bytes=8 * MIB),
        name="combine",
    )(*in_vmem(back), *in_hbm(select))


def per_device(tokens, cotangent, expert_ids, route_weight, gate_weight, up_weight, down_weight):
    experts = lax.axis_size("ep")
    cap = tokens.shape[0] // 32
    depth = tokens.shape[1]
    swap = [(0, 1), (1, 0)]
    ids, weight = expert_ids.T, route_weight.T
    send = route(ids, weight, tokens, cotangent, experts, cap)
    select = selectors(ids, weight, experts, cap)

    def exchange(rows):
        blocks = rows.reshape(experts, 2 * cap, depth)
        return lax.all_to_all(blocks, "ep", split_axis=0, concat_axis=0, tiled=True).reshape(rows.shape)

    def swapped(rows, after=None):
        if after is not None:
            rows, after = lax.optimization_barrier((rows, after))
        return lax.ppermute(rows, "edp", swap), after

    gate, up, down = [
        lax.ppermute(w[0], "edp", swap) for w in (gate_weight, up_weight, down_weight)
    ]
    tok_mine, cot_mine = compact(exchange(send), cap)
    tok_theirs, _ = swapped(tok_mine)
    cot_theirs, tok_theirs = swapped(cot_mine, tok_theirs)
    own_out, other_out, hidden, gate_act, up_act = forward(tok_mine, tok_theirs, gate, up, down)
    arrived_out, cot_theirs = swapped(other_out, cot_theirs)
    own_early, other_early, gate_cot, up_cot = backward(
        cot_mine, cot_theirs, gate, up, down, gate_act, up_act
    )
    arrived_early, arrived_out = swapped(other_early, arrived_out)
    own_late, other_late = late_rows(gate_cot, up_cot, gate, up)
    arrived_late, arrived_early = swapped(other_late, arrived_early)
    back = exchange(
        add_rows(cap, own_out, arrived_out, own_early, arrived_early, own_late, arrived_late)
    )
    hidden, gate_cot, up_cot = [lax.ppermute(a, "edp", swap) for a in (hidden, gate_cot, up_cot)]
    grad_gate, grad_up, grad_down = grads(
        tok_theirs, tok_mine, cot_theirs, cot_mine, hidden, gate_cot, up_cot
    )
    routed_out, token_grad = combine(back, select)
    return (routed_out, token_grad, grad_gate[None], grad_up[None], grad_down[None])


def solution(mesh):
    in_specs = (
        P(("edp", "ep"), None),
        P(("edp", "ep"), None),
        P(("edp", "ep"), None),
        P(("edp", "ep"), None),
        P("ep", None, "edp"),
        P("ep", None, "edp"),
        P("ep", "edp", None),
    )
    out_specs = (
        P(("edp", "ep"), None),
        P(("edp", "ep"), None),
        P("ep", None, "edp"),
        P("ep", None, "edp"),
        P("ep", "edp", None),
    )
    return jax.shard_map(
        per_device, mesh=mesh, in_specs=in_specs, out_specs=out_specs, check_vma=False
    )
```

```python
import jax
import jax.numpy as jnp
from jax import lax
from jax.experimental import pallas as pl
from jax.experimental.pallas import tpu as pltpu
from jax.sharding import PartitionSpec as P

F32 = jnp.float32
BF16 = jnp.bfloat16
MIB = 1024 * 1024
SCOPED = 16 * MIB
ROWS_FIRST = (((0,), (0,)), ((), ()))
COLS = 512
ROUTE_COLS = 3584
COMBINE_COLS = 896


def matmul(a, b, dims=(((1,), (0,)), ((), ()))):
    return lax.dot_general(a, b, dims, preferred_element_type=F32)


WHOLE = pl.BlockSpec(memory_space=pltpu.VMEM)
REMOTE = pl.BlockSpec(memory_space=pl.ANY)


def spread(depth, size=COLS):
    return [pl.ds(j * size, size) for j in range(depth // size)]


def in_hbm(*arrays):
    return [pltpu.with_memory_space_constraint(a, pltpu.HBM) for a in arrays]


def in_vmem(*arrays):
    return [pltpu.with_memory_space_constraint(a, pltpu.VMEM) for a in arrays]


def slots(cap, width, ids_ref, weight_ref, waits):
    tokens = ids_ref.shape[1]
    slot = lax.broadcasted_iota(jnp.int32, (width, tokens), 0)
    expert = slot // (2 * cap)
    place = slot % (2 * cap)
    before = lax.broadcasted_iota(jnp.int32, (tokens, tokens), 0) < lax.broadcasted_iota(
        jnp.int32, (tokens, tokens), 1
    )
    before = jnp.where(before, 1.0, 0.0).astype(BF16)
    for copy in waits:
        copy.wait()
    member = jnp.zeros((width, tokens), F32)
    weight = jnp.zeros((width, tokens), F32)
    for k in range(ids_ref.shape[0]):
        hit = ids_ref[k : k + 1, :] == expert
        member = jnp.where(hit, 1.0, member)
        weight = jnp.where(hit, weight_ref[k : k + 1, :], weight)
    rank = matmul(member.astype(BF16), before)
    chosen = jnp.where(rank == (place % cap).astype(F32), member, 0.0)
    forward = jnp.where(place < cap, chosen, 0.0)
    return forward, chosen - forward, weight


def route_kernel(
    cap, ids_hbm, weight_hbm, tok_hbm, cot_hbm, send_ref, ids_ref, weight_ref, tok_ref, cot_ref, small_sems, sems
):
    parts = spread(tok_hbm.shape[1], ROUTE_COLS)
    small = [
        pltpu.make_async_copy(ids_hbm, ids_ref, small_sems.at[0]),
        pltpu.make_async_copy(weight_hbm, weight_ref, small_sems.at[1]),
    ]
    copies = [
        (
            pltpu.make_async_copy(tok_hbm.at[:, cols], tok_ref.at[:, cols], sems.at[0, j]),
            pltpu.make_async_copy(cot_hbm.at[:, cols], cot_ref.at[:, cols], sems.at[1, j]),
        )
        for j, cols in enumerate(parts)
    ]
    for copy in small:
        copy.start()
    for pair in copies:
        for copy in pair:
            copy.start()
    forward, backward, weight = slots(cap, send_ref.shape[0], ids_ref, weight_ref, small)
    scale = jnp.sum(forward + backward * weight, axis=1, keepdims=True)
    picks = jnp.concatenate([forward, backward], axis=1).astype(BF16)
    for pair, cols in zip(copies, parts):
        for copy in pair:
            copy.wait()
        rows = matmul(picks, jnp.concatenate([tok_ref[:, cols], cot_ref[:, cols]], axis=0))
        send_ref[:, cols] = (rows * scale).astype(BF16)


def route(ids, weight, tokens, cotangent, experts, cap):
    rows, depth = tokens.shape
    width = experts * 2 * cap
    return pl.pallas_call(
        lambda *refs: route_kernel(cap, *refs),
        in_specs=[REMOTE] * 4,
        out_specs=WHOLE,
        out_shape=pltpu.VMEM((width, depth), BF16),
        scratch_shapes=[
            pltpu.VMEM(ids.shape, jnp.int32),
            pltpu.VMEM(weight.shape, F32),
            pltpu.VMEM((rows, depth), BF16),
            pltpu.VMEM((rows, depth), BF16),
            pltpu.SemaphoreType.DMA((2,)),
            pltpu.SemaphoreType.DMA((2, depth // ROUTE_COLS)),
        ],
        compiler_params=pltpu.CompilerParams(vmem_limit_bytes=16 * MIB),
        name="route",
    )(*in_hbm(ids, weight, tokens, cotangent))


def select_kernel(cap, ids_hbm, weight_hbm, select_hbm, ids_ref, weight_ref, select_ref, sems):
    small = [
        pltpu.make_async_copy(ids_hbm, ids_ref, sems.at[0]),
        pltpu.make_async_copy(weight_hbm, weight_ref, sems.at[1]),
    ]
    for copy in small:
        copy.start()
    forward, backward, weight = slots(cap, select_ref.shape[1], ids_ref, weight_ref, small)
    weighted = jnp.transpose(forward * weight)
    high = weighted.astype(BF16)
    count = high.shape[0]
    select_ref[:count] = high
    select_ref[count : 2 * count] = (weighted - high.astype(F32)).astype(BF16)
    select_ref[2 * count :] = jnp.transpose(backward).astype(BF16)
    copy = pltpu.make_async_copy(select_ref, select_hbm, sems.at[2])
    copy.start()
    copy.wait()


def selectors(ids, weight, experts, cap):
    shape = (3 * ids.shape[1], experts * 2 * cap)
    return pl.pallas_call(
        lambda *refs: select_kernel(cap, *refs),
        in_specs=[REMOTE] * 2,
        out_specs=REMOTE,
        out_shape=jax.ShapeDtypeStruct(shape, BF16),
        scratch_shapes=[
            pltpu.VMEM(ids.shape, jnp.int32),
            pltpu.VMEM(weight.shape, F32),
            pltpu.VMEM(shape, BF16),
            pltpu.SemaphoreType.DMA((3,)),
        ],
        compiler_params=pltpu.CompilerParams(vmem_limit_bytes=8 * MIB),
        name="selectors",
    )(*in_hbm(ids, weight))


def compact_kernel(cap, rows_ref, tok_ref, cot_ref):
    groups = rows_ref.shape[0] // (2 * cap)
    half = tok_ref.shape[0]
    for cols in spread(rows_ref.shape[1]):
        both = rows_ref[:, cols].astype(F32).reshape(groups, 2, cap, COLS)
        tok_ref[:, cols] = both[:, 0].reshape(half, COLS).astype(BF16)
        cot_ref[:, cols] = both[:, 1].reshape(half, COLS).astype(BF16)


def compact(rows, cap):
    half, depth = rows.shape[0] // 2, rows.shape[1]
    return pl.pallas_call(
        lambda *refs: compact_kernel(cap, *refs),
        in_specs=[WHOLE],
        out_specs=[WHOLE] * 2,
        out_shape=[pltpu.VMEM((half, depth), BF16)] * 2,
        compiler_params=pltpu.CompilerParams(vmem_limit_bytes=8 * MIB),
        name="compact",
    )(*in_vmem(rows))


def flip_kernel(after_ref, down_ref, flipped_ref):
    for cols in spread(down_ref.shape[1]):
        flipped_ref[cols, :] = jnp.transpose(down_ref[:, cols])


def flip(after, down):
    return pl.pallas_call(
        flip_kernel,
        in_specs=[REMOTE, WHOLE],
        out_specs=WHOLE,
        out_shape=pltpu.VMEM(down.shape[::-1], BF16),
        compiler_params=pltpu.CompilerParams(vmem_limit_bytes=8 * MIB),
        name="flip_down",
    )(*in_vmem(after, down))


def split_store(value, own_ref, other_ref, cols):
    half = own_ref.shape[0]
    own_ref[:, cols] = value[:half].astype(BF16)
    other_ref[:, cols] = value[half:].astype(BF16)


def forward_kernel(
    mine_ref, theirs_ref, gate_ref, up_ref, down_ref,
    own_ref, other_ref, hid_ref, gate_act_ref, up_act_ref, gate_flip_ref, up_flip_ref,
):
    gate_act = jnp.zeros(gate_act_ref.shape, F32)
    up_act = jnp.zeros(up_act_ref.shape, F32)
    for cols in spread(mine_ref.shape[1]):
        rows = jnp.concatenate([mine_ref[:, cols], theirs_ref[:, cols]], axis=0)
        gate_act = gate_act + matmul(rows, gate_ref[cols, :])
        up_act = up_act + matmul(rows, up_ref[cols, :])
        gate_flip_ref[:, cols] = jnp.transpose(gate_ref[cols, :])
    gate_act_ref[...] = gate_act
    up_act_ref[...] = up_act
    hidden = (gate_act * jax.nn.sigmoid(gate_act) * up_act).astype(BF16)
    hid_ref[...] = hidden
    for cols in spread(mine_ref.shape[1]):
        split_store(matmul(hidden, down_ref[:, cols]), own_ref, other_ref, cols)
        up_flip_ref[:, cols] = jnp.transpose(up_ref[cols, :])


def forward(mine, theirs, gate, up, down):
    half, depth = mine.shape
    width = gate.shape[1]
    return pl.pallas_call(
        forward_kernel,
        in_specs=[WHOLE] * 5,
        out_specs=[WHOLE] * 7,
        out_shape=[
            pltpu.VMEM((half, depth), BF16),
            pltpu.VMEM((half, depth), BF16),
            pltpu.VMEM((2 * half, width), BF16),
            pltpu.VMEM((2 * half, width), F32),
            pltpu.VMEM((2 * half, width), F32),
            pltpu.VMEM((width, depth), BF16),
            pltpu.VMEM((width, depth), BF16),
        ],
        compiler_params=pltpu.CompilerParams(vmem_limit_bytes=SCOPED),
        name="expert_forward",
    )(*in_vmem(mine, theirs, gate, up, down))


def row_grads(gate_cot, up_cot, gate_ref, up_ref, own_ref, other_ref, first):
    for j in range(own_ref.shape[1] // COLS):
        cols = pl.ds((first + j) * COLS, COLS)
        back = matmul(gate_cot, gate_ref[:, cols]) + matmul(up_cot, up_ref[:, cols])
        split_store(back, own_ref, other_ref, pl.ds(j * COLS, COLS))


def backward_kernel(
    mine_ref, theirs_ref, gate_ref, up_ref, down_ref, gate_act_ref, up_act_ref,
    own_ref, other_ref, gate_cot_ref, up_cot_ref,
):
    rows = jnp.concatenate([mine_ref[...], theirs_ref[...]], axis=0)
    hidden_cot = matmul(rows, down_ref[...])
    gate_act = gate_act_ref[...]
    sigma = jax.nn.sigmoid(gate_act)
    gate_cot = (hidden_cot * up_act_ref[...] * sigma * (1.0 + gate_act * (1.0 - sigma))).astype(BF16)
    up_cot = (hidden_cot * (gate_act * sigma)).astype(BF16)
    gate_cot_ref[...] = gate_cot
    up_cot_ref[...] = up_cot
    row_grads(gate_cot, up_cot, gate_ref, up_ref, own_ref, other_ref, 0)


def early_cols(depth):
    return depth // COLS * 4 // 7 * COLS


def backward(mine, theirs, gate, up, down, gate_act, up_act):
    half, depth = mine.shape
    width = gate.shape[0]
    early = early_cols(depth)
    return pl.pallas_call(
        backward_kernel,
        in_specs=[WHOLE] * 7,
        out_specs=[WHOLE] * 4,
        out_shape=[pltpu.VMEM((half, early), BF16)] * 2 + [pltpu.VMEM((2 * half, width), BF16)] * 2,
        compiler_params=pltpu.CompilerParams(vmem_limit_bytes=SCOPED),
        name="expert_backward",
    )(*in_vmem(mine, theirs, gate, up, down, gate_act, up_act))


def late_kernel(gate_cot_ref, up_cot_ref, gate_ref, up_ref, own_ref, other_ref):
    first = (gate_ref.shape[1] - own_ref.shape[1]) // COLS
    row_grads(gate_cot_ref[...], up_cot_ref[...], gate_ref, up_ref, own_ref, other_ref, first)


def late_rows(gate_cot, up_cot, gate, up):
    half = gate_cot.shape[0] // 2
    depth = gate.shape[1]
    late = depth - early_cols(depth)
    return pl.pallas_call(
        late_kernel,
        in_specs=[WHOLE] * 4,
        out_specs=[WHOLE] * 2,
        out_shape=[pltpu.VMEM((half, late), BF16)] * 2,
        compiler_params=pltpu.CompilerParams(vmem_limit_bytes=8 * MIB),
        name="late_rows",
    )(*in_vmem(gate_cot, up_cot, gate, up))


def add_kernel(cap, first, own_out, arrived_out, own_ref, arrived_ref, *refs):
    out_hbm, out_ref, sems = refs[-3:]
    rows = out_ref.shape[0]
    groups = rows // (2 * cap)
    copies = []
    for j, here in enumerate(spread(out_ref.shape[1])):
        cols = pl.ds((first + j) * COLS, COLS)
        out = own_out[:, cols].astype(F32) + arrived_out[:, cols].astype(F32)
        grad = own_ref[:, here].astype(F32) + arrived_ref[:, here].astype(F32)
        both = jnp.concatenate([out.reshape(groups, cap, COLS), grad.reshape(groups, cap, COLS)], axis=1)
        out_ref[:, here] = both.reshape(rows, COLS).astype(BF16)
        copies.append(pltpu.make_async_copy(out_ref.at[:, here], out_hbm.at[:, cols], sems.at[j]))
        copies[j].start()
    for copy in copies:
        copy.wait()


def add_rows(cap, first, own_out, arrived_out, own, arrived, filled=None):
    half, depth = own_out.shape
    cols = own.shape[1]
    more = [] if filled is None else in_hbm(filled)
    return pl.pallas_call(
        lambda *refs: add_kernel(cap, first, *refs),
        in_specs=[WHOLE] * 4 + [REMOTE] * len(more),
        out_specs=REMOTE,
        out_shape=pltpu.HBM((2 * half, depth), BF16),
        scratch_shapes=[pltpu.VMEM((2 * half, cols), BF16), pltpu.SemaphoreType.DMA((cols // COLS,))],
        input_output_aliases={4: 0} if more else {},
        compiler_params=pltpu.CompilerParams(vmem_limit_bytes=16 * MIB),
        name="add_late" if more else "add_early",
    )(*in_vmem(own_out, arrived_out, own, arrived), *more)


def grads_kernel(
    tok_mine, tok_theirs, cot_mine, cot_theirs, hid_ref, gate_cot_ref, up_cot_ref, gate_ref, up_ref, down_ref
):
    cols = pl.ds(pl.multiple_of(pl.program_id(0) * COLS, COLS), COLS)
    width = gate_ref.shape[1]
    pair = jnp.concatenate([gate_cot_ref[...], up_cot_ref[...]], axis=1)
    tokens = jnp.concatenate([tok_mine[:, cols], tok_theirs[:, cols]], axis=0)
    both = matmul(tokens, pair, ROWS_FIRST)
    gate_ref[...] = both[:, :width].astype(BF16)
    up_ref[...] = both[:, width:].astype(BF16)
    cotangent = jnp.concatenate([cot_mine[:, cols], cot_theirs[:, cols]], axis=0)
    down_ref[...] = matmul(hid_ref[...], cotangent, ROWS_FIRST).astype(BF16)


def grads(tok_mine, tok_theirs, cot_mine, cot_theirs, hidden, gate_cot, up_cot):
    depth = tok_mine.shape[1]
    width = hidden.shape[1]
    return pl.pallas_call(
        grads_kernel,
        grid=(depth // COLS,),
        in_specs=[WHOLE] * 7,
        out_specs=[
            pl.BlockSpec((COLS, width), lambda j: (j, 0)),
            pl.BlockSpec((COLS, width), lambda j: (j, 0)),
            pl.BlockSpec((width, COLS), lambda j: (0, j)),
        ],
        out_shape=[
            jax.ShapeDtypeStruct((depth, width), BF16),
            jax.ShapeDtypeStruct((depth, width), BF16),
            jax.ShapeDtypeStruct((width, depth), BF16),
        ],
        compiler_params=pltpu.CompilerParams(vmem_limit_bytes=SCOPED),
        name="weight_grads",
    )(*in_vmem(tok_mine, tok_theirs, cot_mine, cot_theirs, hidden, gate_cot, up_cot))


def combine_kernel(back_ref, select_ref, out_hbm, grad_hbm, out_ref, grad_ref, sems):
    count = out_ref.shape[0]
    copies = []
    for j, cols in enumerate(spread(back_ref.shape[1], COMBINE_COLS)):
        sums = matmul(select_ref[...], back_ref[:, cols])
        out_ref[:, cols] = (sums[:count] + sums[count : 2 * count]).astype(BF16)
        grad_ref[:, cols] = sums[2 * count :].astype(BF16)
        pair = [
            pltpu.make_async_copy(out_ref.at[:, cols], out_hbm.at[:, cols], sems.at[0, j]),
            pltpu.make_async_copy(grad_ref.at[:, cols], grad_hbm.at[:, cols], sems.at[1, j]),
        ]
        for copy in pair:
            copy.start()
        copies.extend(pair)
    for copy in copies:
        copy.wait()


def combine(back, select):
    width, depth = back.shape
    rows = select.shape[0] // 3
    return pl.pallas_call(
        combine_kernel,
        in_specs=[WHOLE, WHOLE],
        out_specs=[REMOTE, REMOTE],
        out_shape=[pltpu.HBM((rows, depth), BF16)] * 2,
        scratch_shapes=[
            pltpu.VMEM((rows, depth), BF16),
            pltpu.VMEM((rows, depth), BF16),
            pltpu.SemaphoreType.DMA((2, depth // COMBINE_COLS)),
        ],
        compiler_params=pltpu.CompilerParams(vmem_limit_bytes=8 * MIB),
        name="combine",
    )(*in_vmem(back), select)


def per_device(tokens, cotangent, expert_ids, route_weight, gate_weight, up_weight, down_weight):
    experts = lax.axis_size("ep")
    cap = tokens.shape[0] // 32
    depth = tokens.shape[1]
    swap = [(0, 1), (1, 0)]
    ids, weight = expert_ids.T, route_weight.T
    send = route(ids, weight, tokens, cotangent, experts, cap)
    select = selectors(ids, weight, experts, cap)

    def exchange(rows):
        blocks = rows.reshape(experts, 2 * cap, depth)
        return lax.all_to_all(blocks, "ep", split_axis=0, concat_axis=0, tiled=True).reshape(rows.shape)

    def swapped(rows, after=None):
        if after is not None:
            rows, after = lax.optimization_barrier((rows, after))
        return lax.ppermute(rows, "edp", swap), after

    gate, up, down = [
        lax.ppermute(w[0], "edp", swap) for w in (gate_weight, up_weight, down_weight)
    ]
    tok_mine, cot_mine = compact(exchange(send), cap)
    tok_theirs, _ = swapped(tok_mine)
    down_flip = flip(tok_mine, down)
    cot_theirs, (tok_theirs, down_flip) = swapped(cot_mine, (tok_theirs, down_flip))
    own_out, other_out, hidden, gate_act, up_act, gate_flip, up_flip = forward(
        tok_mine, tok_theirs, gate, up, down
    )
    arrived_out, cot_theirs = swapped(other_out, cot_theirs)
    own_early, other_early, gate_cot, up_cot = backward(
        cot_mine, cot_theirs, gate_flip, up_flip, down_flip, gate_act, up_act
    )
    arrived_early, _ = swapped(other_early)
    own_late, other_late = late_rows(gate_cot, up_cot, gate_flip, up_flip)
    arrived_late, _ = swapped(other_late)
    sums = add_rows(cap, 0, own_out, arrived_out, own_early, arrived_early)
    sums = add_rows(cap, own_early.shape[1] // COLS, own_out, arrived_out, own_late, arrived_late, sums)
    back = exchange(sums)
    hidden, gate_cot, up_cot = [lax.ppermute(a, "edp", swap) for a in (hidden, gate_cot, up_cot)]
    grad_gate, grad_up, grad_down = grads(
        tok_theirs, tok_mine, cot_theirs, cot_mine, hidden, gate_cot, up_cot
    )
    routed_out, token_grad = combine(back, select)
    return (routed_out, token_grad, grad_gate[None], grad_up[None], grad_down[None])


def solution(mesh):
    in_specs = (
        P(("edp", "ep"), None),
        P(("edp", "ep"), None),
        P(("edp", "ep"), None),
        P(("edp", "ep"), None),
        P("ep", None, "edp"),
        P("ep", None, "edp"),
        P("ep", "edp", None),
    )
    out_specs = (
        P(("edp", "ep"), None),
        P(("edp", "ep"), None),
        P("ep", None, "edp"),
        P("ep", None, "edp"),
        P("ep", "edp", None),
    )
    return jax.shard_map(
        per_device, mesh=mesh, in_specs=in_specs, out_specs=out_specs, check_vma=False
    )
```

```python
import jax
import jax.numpy as jnp
from jax import lax
from jax.experimental import pallas as pl
from jax.experimental.pallas import tpu as pltpu
from jax.sharding import PartitionSpec as P

F32 = jnp.float32
BF16 = jnp.bfloat16
MIB = 1024 * 1024
SCOPED = 16 * MIB
ROWS_FIRST = (((0,), (0,)), ((), ()))
COLS = 512
ROUTE_COLS = 3584
COMBINE_COLS = 896


def matmul(a, b, dims=(((1,), (0,)), ((), ()))):
    return lax.dot_general(a, b, dims, preferred_element_type=F32)


WHOLE = pl.BlockSpec(memory_space=pltpu.VMEM)
REMOTE = pl.BlockSpec(memory_space=pl.ANY)


def spread(depth, size=COLS):
    return [pl.ds(j * size, size) for j in range(depth // size)]


def in_hbm(*arrays):
    return [pltpu.with_memory_space_constraint(a, pltpu.HBM) for a in arrays]


def in_vmem(*arrays):
    return [pltpu.with_memory_space_constraint(a, pltpu.VMEM) for a in arrays]


def far_corner(experts):
    return experts // 2 + experts // 8


def slots(cap, width, ids_ref, weight_ref, waits):
    tokens = ids_ref.shape[1]
    slot = lax.broadcasted_iota(jnp.int32, (width, tokens), 0)
    expert = (slot // (2 * cap)) ^ (lax.axis_index("edp") * far_corner(width // (2 * cap)))
    place = slot % (2 * cap)
    before = lax.broadcasted_iota(jnp.int32, (tokens, tokens), 0) < lax.broadcasted_iota(
        jnp.int32, (tokens, tokens), 1
    )
    before = jnp.where(before, 1.0, 0.0).astype(BF16)
    for copy in waits:
        copy.wait()
    member = jnp.zeros((width, tokens), F32)
    weight = jnp.zeros((width, tokens), F32)
    for k in range(ids_ref.shape[0]):
        hit = ids_ref[k : k + 1, :] == expert
        member = jnp.where(hit, 1.0, member)
        weight = jnp.where(hit, weight_ref[k : k + 1, :], weight)
    rank = matmul(member.astype(BF16), before)
    chosen = jnp.where(rank == (place % cap).astype(F32), member, 0.0)
    forward = jnp.where(place < cap, chosen, 0.0)
    return forward, chosen - forward, weight


def route_kernel(
    cap, ids_hbm, weight_hbm, tok_hbm, cot_hbm, send_ref, ids_ref, weight_ref, tok_ref, cot_ref, small_sems, sems
):
    parts = spread(tok_hbm.shape[1], ROUTE_COLS)
    small = [
        pltpu.make_async_copy(ids_hbm, ids_ref, small_sems.at[0]),
        pltpu.make_async_copy(weight_hbm, weight_ref, small_sems.at[1]),
    ]
    copies = [
        (
            pltpu.make_async_copy(tok_hbm.at[:, cols], tok_ref.at[:, cols], sems.at[0, j]),
            pltpu.make_async_copy(cot_hbm.at[:, cols], cot_ref.at[:, cols], sems.at[1, j]),
        )
        for j, cols in enumerate(parts)
    ]
    for copy in small:
        copy.start()
    for pair in copies:
        for copy in pair:
            copy.start()
    forward, backward, weight = slots(cap, send_ref.shape[0], ids_ref, weight_ref, small)
    scale = jnp.sum(forward + backward * weight, axis=1, keepdims=True)
    picks = jnp.concatenate([forward, backward], axis=1).astype(BF16)
    for pair, cols in zip(copies, parts):
        for copy in pair:
            copy.wait()
        rows = matmul(picks, jnp.concatenate([tok_ref[:, cols], cot_ref[:, cols]], axis=0))
        send_ref[:, cols] = (rows * scale).astype(BF16)


def route(ids, weight, tokens, cotangent, experts, cap):
    rows, depth = tokens.shape
    width = experts * 2 * cap
    return pl.pallas_call(
        lambda *refs: route_kernel(cap, *refs),
        in_specs=[REMOTE] * 4,
        out_specs=WHOLE,
        out_shape=pltpu.VMEM((width, depth), BF16),
        scratch_shapes=[
            pltpu.VMEM(ids.shape, jnp.int32),
            pltpu.VMEM(weight.shape, F32),
            pltpu.VMEM((rows, depth), BF16),
            pltpu.VMEM((rows, depth), BF16),
            pltpu.SemaphoreType.DMA((2,)),
            pltpu.SemaphoreType.DMA((2, depth // ROUTE_COLS)),
        ],
        compiler_params=pltpu.CompilerParams(vmem_limit_bytes=16 * MIB),
        name="route",
    )(*in_hbm(ids, weight, tokens, cotangent))


def select_kernel(cap, ids_hbm, weight_hbm, select_hbm, ids_ref, weight_ref, select_ref, sems):
    small = [
        pltpu.make_async_copy(ids_hbm, ids_ref, sems.at[0]),
        pltpu.make_async_copy(weight_hbm, weight_ref, sems.at[1]),
    ]
    for copy in small:
        copy.start()
    forward, backward, weight = slots(cap, select_ref.shape[1], ids_ref, weight_ref, small)
    weighted = jnp.transpose(forward * weight)
    high = weighted.astype(BF16)
    count = high.shape[0]
    select_ref[:count] = high
    select_ref[count : 2 * count] = (weighted - high.astype(F32)).astype(BF16)
    select_ref[2 * count :] = jnp.transpose(backward).astype(BF16)
    copy = pltpu.make_async_copy(select_ref, select_hbm, sems.at[2])
    copy.start()
    copy.wait()


def selectors(ids, weight, experts, cap):
    shape = (3 * ids.shape[1], experts * 2 * cap)
    return pl.pallas_call(
        lambda *refs: select_kernel(cap, *refs),
        in_specs=[REMOTE] * 2,
        out_specs=REMOTE,
        out_shape=jax.ShapeDtypeStruct(shape, BF16),
        scratch_shapes=[
            pltpu.VMEM(ids.shape, jnp.int32),
            pltpu.VMEM(weight.shape, F32),
            pltpu.VMEM(shape, BF16),
            pltpu.SemaphoreType.DMA((3,)),
        ],
        compiler_params=pltpu.CompilerParams(vmem_limit_bytes=8 * MIB),
        name="selectors",
    )(*in_hbm(ids, weight))


def compact_kernel(cap, rows_ref, tok_ref, cot_ref):
    groups = rows_ref.shape[0] // (2 * cap)
    half = tok_ref.shape[0]
    for cols in spread(rows_ref.shape[1]):
        both = rows_ref[:, cols].astype(F32).reshape(groups, 2, cap, COLS)
        tok_ref[:, cols] = both[:, 0].reshape(half, COLS).astype(BF16)
        cot_ref[:, cols] = both[:, 1].reshape(half, COLS).astype(BF16)


def compact(rows, cap):
    half, depth = rows.shape[0] // 2, rows.shape[1]
    return pl.pallas_call(
        lambda *refs: compact_kernel(cap, *refs),
        in_specs=[WHOLE],
        out_specs=[WHOLE] * 2,
        out_shape=[pltpu.VMEM((half, depth), BF16)] * 2,
        compiler_params=pltpu.CompilerParams(vmem_limit_bytes=8 * MIB),
        name="compact",
    )(*in_vmem(rows))


def flip_kernel(after_ref, down_ref, flipped_ref):
    for cols in spread(down_ref.shape[1]):
        flipped_ref[cols, :] = jnp.transpose(down_ref[:, cols])


def flip(after, down):
    return pl.pallas_call(
        flip_kernel,
        in_specs=[REMOTE, WHOLE],
        out_specs=WHOLE,
        out_shape=pltpu.VMEM(down.shape[::-1], BF16),
        compiler_params=pltpu.CompilerParams(vmem_limit_bytes=8 * MIB),
        name="flip_down",
    )(*in_vmem(after, down))


def split_store(value, own_ref, other_ref, cols):
    half = own_ref.shape[0]
    own_ref[:, cols] = value[:half].astype(BF16)
    other_ref[:, cols] = value[half:].astype(BF16)


def forward_kernel(
    mine_ref, theirs_ref, gate_ref, up_ref, down_ref,
    own_ref, other_ref, hid_ref, gate_act_ref, up_act_ref, gate_flip_ref, up_flip_ref,
):
    gate_act = jnp.zeros(gate_act_ref.shape, F32)
    up_act = jnp.zeros(up_act_ref.shape, F32)
    for cols in spread(mine_ref.shape[1]):
        rows = jnp.concatenate([mine_ref[:, cols], theirs_ref[:, cols]], axis=0)
        gate_act = gate_act + matmul(rows, gate_ref[cols, :])
        up_act = up_act + matmul(rows, up_ref[cols, :])
        gate_flip_ref[:, cols] = jnp.transpose(gate_ref[cols, :])
    gate_act_ref[...] = gate_act
    up_act_ref[...] = up_act
    hidden = (gate_act * jax.nn.sigmoid(gate_act) * up_act).astype(BF16)
    hid_ref[...] = hidden
    for cols in spread(mine_ref.shape[1]):
        split_store(matmul(hidden, down_ref[:, cols]), own_ref, other_ref, cols)
        up_flip_ref[:, cols] = jnp.transpose(up_ref[cols, :])


def forward(mine, theirs, gate, up, down):
    half, depth = mine.shape
    width = gate.shape[1]
    return pl.pallas_call(
        forward_kernel,
        in_specs=[WHOLE] * 5,
        out_specs=[WHOLE] * 7,
        out_shape=[
            pltpu.VMEM((half, depth), BF16),
            pltpu.VMEM((half, depth), BF16),
            pltpu.VMEM((2 * half, width), BF16),
            pltpu.VMEM((2 * half, width), F32),
            pltpu.VMEM((2 * half, width), F32),
            pltpu.VMEM((width, depth), BF16),
            pltpu.VMEM((width, depth), BF16),
        ],
        compiler_params=pltpu.CompilerParams(vmem_limit_bytes=SCOPED),
        name="expert_forward",
    )(*in_vmem(mine, theirs, gate, up, down))


def row_grads(gate_cot, up_cot, gate_ref, up_ref, own_ref, other_ref, first):
    for j in range(own_ref.shape[1] // COLS):
        cols = pl.ds((first + j) * COLS, COLS)
        back = matmul(gate_cot, gate_ref[:, cols]) + matmul(up_cot, up_ref[:, cols])
        split_store(back, own_ref, other_ref, pl.ds(j * COLS, COLS))


def backward_kernel(
    mine_ref, theirs_ref, gate_ref, up_ref, down_ref, gate_act_ref, up_act_ref,
    own_ref, other_ref, gate_cot_ref, up_cot_ref,
):
    rows = jnp.concatenate([mine_ref[...], theirs_ref[...]], axis=0)
    hidden_cot = matmul(rows, down_ref[...])
    gate_act = gate_act_ref[...]
    sigma = jax.nn.sigmoid(gate_act)
    gate_cot = (hidden_cot * up_act_ref[...] * sigma * (1.0 + gate_act * (1.0 - sigma))).astype(BF16)
    up_cot = (hidden_cot * (gate_act * sigma)).astype(BF16)
    gate_cot_ref[...] = gate_cot
    up_cot_ref[...] = up_cot
    row_grads(gate_cot, up_cot, gate_ref, up_ref, own_ref, other_ref, 0)


def early_cols(depth):
    return depth // COLS * 4 // 7 * COLS


def backward(mine, theirs, gate, up, down, gate_act, up_act):
    half, depth = mine.shape
    width = gate.shape[0]
    early = early_cols(depth)
    return pl.pallas_call(
        backward_kernel,
        in_specs=[WHOLE] * 7,
        out_specs=[WHOLE] * 4,
        out_shape=[pltpu.VMEM((half, early), BF16)] * 2 + [pltpu.VMEM((2 * half, width), BF16)] * 2,
        compiler_params=pltpu.CompilerParams(vmem_limit_bytes=SCOPED),
        name="expert_backward",
    )(*in_vmem(mine, theirs, gate, up, down, gate_act, up_act))


def late_kernel(gate_cot_ref, up_cot_ref, gate_ref, up_ref, own_ref, other_ref):
    first = (gate_ref.shape[1] - own_ref.shape[1]) // COLS
    row_grads(gate_cot_ref[...], up_cot_ref[...], gate_ref, up_ref, own_ref, other_ref, first)


def late_rows(gate_cot, up_cot, gate, up):
    half = gate_cot.shape[0] // 2
    depth = gate.shape[1]
    late = depth - early_cols(depth)
    return pl.pallas_call(
        late_kernel,
        in_specs=[WHOLE] * 4,
        out_specs=[WHOLE] * 2,
        out_shape=[pltpu.VMEM((half, late), BF16)] * 2,
        compiler_params=pltpu.CompilerParams(vmem_limit_bytes=8 * MIB),
        name="late_rows",
    )(*in_vmem(gate_cot, up_cot, gate, up))


def add_kernel(cap, first, own_out, arrived_out, own_ref, arrived_ref, *refs):
    out_hbm, out_ref, sems = refs[-3:]
    rows = out_ref.shape[0]
    groups = rows // (2 * cap)
    copies = []
    for j, here in enumerate(spread(out_ref.shape[1])):
        cols = pl.ds((first + j) * COLS, COLS)
        out = own_out[:, cols].astype(F32) + arrived_out[:, cols].astype(F32)
        grad = own_ref[:, here].astype(F32) + arrived_ref[:, here].astype(F32)
        both = jnp.concatenate([out.reshape(groups, cap, COLS), grad.reshape(groups, cap, COLS)], axis=1)
        out_ref[:, here] = both.reshape(rows, COLS).astype(BF16)
        copies.append(pltpu.make_async_copy(out_ref.at[:, here], out_hbm.at[:, cols], sems.at[j]))
        copies[j].start()
    for copy in copies:
        copy.wait()


def add_rows(cap, first, own_out, arrived_out, own, arrived, filled=None):
    half, depth = own_out.shape
    cols = own.shape[1]
    more = [] if filled is None else in_hbm(filled)
    return pl.pallas_call(
        lambda *refs: add_kernel(cap, first, *refs),
        in_specs=[WHOLE] * 4 + [REMOTE] * len(more),
        out_specs=REMOTE,
        out_shape=pltpu.HBM((2 * half, depth), BF16),
        scratch_shapes=[pltpu.VMEM((2 * half, cols), BF16), pltpu.SemaphoreType.DMA((cols // COLS,))],
        input_output_aliases={4: 0} if more else {},
        compiler_params=pltpu.CompilerParams(vmem_limit_bytes=16 * MIB),
        name="add_late" if more else "add_early",
    )(*in_vmem(own_out, arrived_out, own, arrived), *more)


def grads_kernel(
    tok_mine, tok_theirs, cot_mine, cot_theirs, hid_ref, gate_cot_ref, up_cot_ref, gate_ref, up_ref, down_ref
):
    cols = pl.ds(pl.multiple_of(pl.program_id(0) * COLS, COLS), COLS)
    width = gate_ref.shape[1]
    pair = jnp.concatenate([gate_cot_ref[...], up_cot_ref[...]], axis=1)
    tokens = jnp.concatenate([tok_mine[:, cols], tok_theirs[:, cols]], axis=0)
    both = matmul(tokens, pair, ROWS_FIRST)
    gate_ref[...] = both[:, :width].astype(BF16)
    up_ref[...] = both[:, width:].astype(BF16)
    cotangent = jnp.concatenate([cot_mine[:, cols], cot_theirs[:, cols]], axis=0)
    down_ref[...] = matmul(hid_ref[...], cotangent, ROWS_FIRST).astype(BF16)


def grads(tok_mine, tok_theirs, cot_mine, cot_theirs, hidden, gate_cot, up_cot):
    depth = tok_mine.shape[1]
    width = hidden.shape[1]
    return pl.pallas_call(
        grads_kernel,
        grid=(depth // COLS,),
        in_specs=[WHOLE] * 7,
        out_specs=[
            pl.BlockSpec((COLS, width), lambda j: (j, 0)),
            pl.BlockSpec((COLS, width), lambda j: (j, 0)),
            pl.BlockSpec((width, COLS), lambda j: (0, j)),
        ],
        out_shape=[
            jax.ShapeDtypeStruct((depth, width), BF16),
            jax.ShapeDtypeStruct((depth, width), BF16),
            jax.ShapeDtypeStruct((width, depth), BF16),
        ],
        compiler_params=pltpu.CompilerParams(vmem_limit_bytes=SCOPED),
        name="weight_grads",
    )(*in_vmem(tok_mine, tok_theirs, cot_mine, cot_theirs, hidden, gate_cot, up_cot))


def combine_kernel(back_ref, select_ref, out_hbm, grad_hbm, out_ref, grad_ref, sems):
    count = out_ref.shape[0]
    copies = []
    for j, cols in enumerate(spread(back_ref.shape[1], COMBINE_COLS)):
        sums = matmul(select_ref[...], back_ref[:, cols])
        out_ref[:, cols] = (sums[:count] + sums[count : 2 * count]).astype(BF16)
        grad_ref[:, cols] = sums[2 * count :].astype(BF16)
        pair = [
            pltpu.make_async_copy(out_ref.at[:, cols], out_hbm.at[:, cols], sems.at[0, j]),
            pltpu.make_async_copy(grad_ref.at[:, cols], grad_hbm.at[:, cols], sems.at[1, j]),
        ]
        for copy in pair:
            copy.start()
        copies.extend(pair)
    for copy in copies:
        copy.wait()


def combine(back, select):
    width, depth = back.shape
    rows = select.shape[0] // 3
    return pl.pallas_call(
        combine_kernel,
        in_specs=[WHOLE, WHOLE],
        out_specs=[REMOTE, REMOTE],
        out_shape=[pltpu.HBM((rows, depth), BF16)] * 2,
        scratch_shapes=[
            pltpu.VMEM((rows, depth), BF16),
            pltpu.VMEM((rows, depth), BF16),
            pltpu.SemaphoreType.DMA((2, depth // COMBINE_COLS)),
        ],
        compiler_params=pltpu.CompilerParams(vmem_limit_bytes=8 * MIB),
        name="combine",
    )(*in_vmem(back), select)


def per_device(tokens, cotangent, expert_ids, route_weight, gate_weight, up_weight, down_weight):
    experts = lax.axis_size("ep")
    cap = tokens.shape[0] // 32
    depth = tokens.shape[1]
    swap = [(0, 1), (1, 0)]
    ids, weight = expert_ids.T, route_weight.T
    send = route(ids, weight, tokens, cotangent, experts, cap)
    select = selectors(ids, weight, experts, cap)

    orders = [list(range(experts)), [experts + (i ^ far_corner(experts)) for i in range(experts)]]

    def exchange(rows):
        blocks = rows.reshape(experts, 2 * cap, depth)
        return lax.all_to_all(
            blocks, ("edp", "ep"), split_axis=0, concat_axis=0, tiled=True, axis_index_groups=orders
        ).reshape(rows.shape)

    def swapped(rows, after=None):
        if after is not None:
            rows, after = lax.optimization_barrier((rows, after))
        return lax.ppermute(rows, "edp", swap), after

    gate, up, down = [
        lax.ppermute(w[0], "edp", swap) for w in (gate_weight, up_weight, down_weight)
    ]
    tok_mine, cot_mine = compact(exchange(send), cap)
    tok_theirs, _ = swapped(tok_mine)
    down_flip = flip(tok_mine, down)
    cot_theirs, (tok_theirs, down_flip) = swapped(cot_mine, (tok_theirs, down_flip))
    own_out, other_out, hidden, gate_act, up_act, gate_flip, up_flip = forward(
        tok_mine, tok_theirs, gate, up, down
    )
    arrived_out, cot_theirs = swapped(other_out, cot_theirs)
    own_early, other_early, gate_cot, up_cot = backward(
        cot_mine, cot_theirs, gate_flip, up_flip, down_flip, gate_act, up_act
    )
    arrived_early, _ = swapped(other_early)
    own_late, other_late = late_rows(gate_cot, up_cot, gate_flip, up_flip)
    arrived_late, _ = swapped(other_late)
    sums = add_rows(cap, 0, own_out, arrived_out, own_early, arrived_early)
    sums = add_rows(cap, own_early.shape[1] // COLS, own_out, arrived_out, own_late, arrived_late, sums)
    back = exchange(sums)
    hidden, gate_cot, up_cot = [lax.ppermute(a, "edp", swap) for a in (hidden, gate_cot, up_cot)]
    grad_gate, grad_up, grad_down = grads(
        tok_theirs, tok_mine, cot_theirs, cot_mine, hidden, gate_cot, up_cot
    )
    routed_out, token_grad = combine(back, select)
    return (routed_out, token_grad, grad_gate[None], grad_up[None], grad_down[None])


def solution(mesh):
    in_specs = (
        P(("edp", "ep"), None),
        P(("edp", "ep"), None),
        P(("edp", "ep"), None),
        P(("edp", "ep"), None),
        P("ep", None, "edp"),
        P("ep", None, "edp"),
        P("ep", "edp", None),
    )
    out_specs = (
        P(("edp", "ep"), None),
        P(("edp", "ep"), None),
        P("ep", None, "edp"),
        P("ep", None, "edp"),
        P("ep", "edp", None),
    )
    return jax.shard_map(
        per_device, mesh=mesh, in_specs=in_specs, out_specs=out_specs, check_vma=False
    )
```

```python
import jax
import jax.numpy as jnp
from jax import lax
from jax.experimental import pallas as pl
from jax.experimental.pallas import tpu as pltpu
from jax.sharding import PartitionSpec as P

F32 = jnp.float32
BF16 = jnp.bfloat16
MIB = 1024 * 1024
SCOPED = 16 * MIB
ROWS_FIRST = (((0,), (0,)), ((), ()))
COLS = 512
ROUTE_COLS = 3584
COMBINE_COLS = 896


def matmul(a, b, dims=(((1,), (0,)), ((), ()))):
    return lax.dot_general(a, b, dims, preferred_element_type=F32)


WHOLE = pl.BlockSpec(memory_space=pltpu.VMEM)
REMOTE = pl.BlockSpec(memory_space=pl.ANY)


def spread(depth, size=COLS):
    return [pl.ds(j * size, size) for j in range(depth // size)]


def in_hbm(*arrays):
    return [pltpu.with_memory_space_constraint(a, pltpu.HBM) for a in arrays]


def in_vmem(*arrays):
    return [pltpu.with_memory_space_constraint(a, pltpu.VMEM) for a in arrays]


def far_corner(experts):
    return experts // 2 + experts // 8


def slots(cap, width, ids_ref, weight_ref, waits):
    tokens = ids_ref.shape[1]
    slot = lax.broadcasted_iota(jnp.int32, (width, tokens), 0)
    expert = (slot // (2 * cap)) ^ (lax.axis_index("edp") * far_corner(width // (2 * cap)))
    place = slot % (2 * cap)
    before = lax.broadcasted_iota(jnp.int32, (tokens, tokens), 0) < lax.broadcasted_iota(
        jnp.int32, (tokens, tokens), 1
    )
    before = jnp.where(before, 1.0, 0.0).astype(BF16)
    for copy in waits:
        copy.wait()
    member = jnp.zeros((width, tokens), F32)
    weight = jnp.zeros((width, tokens), F32)
    for k in range(ids_ref.shape[0]):
        hit = ids_ref[k : k + 1, :] == expert
        member = jnp.where(hit, 1.0, member)
        weight = jnp.where(hit, weight_ref[k : k + 1, :], weight)
    rank = matmul(member.astype(BF16), before)
    chosen = jnp.where(rank == (place % cap).astype(F32), member, 0.0)
    forward = jnp.where(place < cap, chosen, 0.0)
    return forward, chosen - forward, weight


def route_kernel(
    cap, ids_hbm, weight_hbm, tok_hbm, cot_hbm, send_ref, ids_ref, weight_ref, tok_ref, cot_ref, small_sems, sems
):
    parts = spread(tok_hbm.shape[1], ROUTE_COLS)
    small = [
        pltpu.make_async_copy(ids_hbm, ids_ref, small_sems.at[0]),
        pltpu.make_async_copy(weight_hbm, weight_ref, small_sems.at[1]),
    ]
    copies = [
        (
            pltpu.make_async_copy(tok_hbm.at[:, cols], tok_ref.at[:, cols], sems.at[0, j]),
            pltpu.make_async_copy(cot_hbm.at[:, cols], cot_ref.at[:, cols], sems.at[1, j]),
        )
        for j, cols in enumerate(parts)
    ]
    for copy in small:
        copy.start()
    for pair in copies:
        for copy in pair:
            copy.start()
    forward, backward, weight = slots(cap, send_ref.shape[0], ids_ref, weight_ref, small)
    scale = jnp.sum(forward + backward * weight, axis=1, keepdims=True)
    picks = jnp.concatenate([forward, backward], axis=1).astype(BF16)
    for pair, cols in zip(copies, parts):
        for copy in pair:
            copy.wait()
        rows = matmul(picks, jnp.concatenate([tok_ref[:, cols], cot_ref[:, cols]], axis=0))
        send_ref[:, cols] = (rows * scale).astype(BF16)


def route(ids, weight, tokens, cotangent, experts, cap):
    rows, depth = tokens.shape
    width = experts * 2 * cap
    return pl.pallas_call(
        lambda *refs: route_kernel(cap, *refs),
        in_specs=[REMOTE] * 4,
        out_specs=WHOLE,
        out_shape=pltpu.VMEM((width, depth), BF16),
        scratch_shapes=[
            pltpu.VMEM(ids.shape, jnp.int32),
            pltpu.VMEM(weight.shape, F32),
            pltpu.VMEM((rows, depth), BF16),
            pltpu.VMEM((rows, depth), BF16),
            pltpu.SemaphoreType.DMA((2,)),
            pltpu.SemaphoreType.DMA((2, depth // ROUTE_COLS)),
        ],
        compiler_params=pltpu.CompilerParams(vmem_limit_bytes=16 * MIB),
        name="route",
    )(*in_hbm(ids, weight, tokens, cotangent))


def select_kernel(cap, ids_hbm, weight_hbm, select_hbm, ids_ref, weight_ref, select_ref, sems):
    small = [
        pltpu.make_async_copy(ids_hbm, ids_ref, sems.at[0]),
        pltpu.make_async_copy(weight_hbm, weight_ref, sems.at[1]),
    ]
    for copy in small:
        copy.start()
    forward, backward, weight = slots(cap, select_ref.shape[1], ids_ref, weight_ref, small)
    weighted = jnp.transpose(forward * weight)
    high = weighted.astype(BF16)
    count = high.shape[0]
    select_ref[:count] = high
    select_ref[count : 2 * count] = (weighted - high.astype(F32)).astype(BF16)
    select_ref[2 * count :] = jnp.transpose(backward).astype(BF16)
    copy = pltpu.make_async_copy(select_ref, select_hbm, sems.at[2])
    copy.start()
    copy.wait()


def selectors(ids, weight, experts, cap):
    shape = (3 * ids.shape[1], experts * 2 * cap)
    return pl.pallas_call(
        lambda *refs: select_kernel(cap, *refs),
        in_specs=[REMOTE] * 2,
        out_specs=REMOTE,
        out_shape=jax.ShapeDtypeStruct(shape, BF16),
        scratch_shapes=[
            pltpu.VMEM(ids.shape, jnp.int32),
            pltpu.VMEM(weight.shape, F32),
            pltpu.VMEM(shape, BF16),
            pltpu.SemaphoreType.DMA((3,)),
        ],
        compiler_params=pltpu.CompilerParams(vmem_limit_bytes=8 * MIB),
        name="selectors",
    )(*in_hbm(ids, weight))


def compact_kernel(cap, rows_ref, tok_ref, cot_ref):
    groups = rows_ref.shape[0] // (2 * cap)
    half = tok_ref.shape[0]
    for cols in spread(rows_ref.shape[1]):
        both = rows_ref[:, cols].astype(F32).reshape(groups, 2, cap, COLS)
        tok_ref[:, cols] = both[:, 0].reshape(half, COLS).astype(BF16)
        cot_ref[:, cols] = both[:, 1].reshape(half, COLS).astype(BF16)


def compact(rows, cap):
    half, depth = rows.shape[0] // 2, rows.shape[1]
    return pl.pallas_call(
        lambda *refs: compact_kernel(cap, *refs),
        in_specs=[WHOLE],
        out_specs=[WHOLE] * 2,
        out_shape=[pltpu.VMEM((half, depth), BF16)] * 2,
        compiler_params=pltpu.CompilerParams(vmem_limit_bytes=8 * MIB),
        name="compact",
    )(*in_vmem(rows))


def flip_kernel(after_ref, down_ref, flipped_ref):
    for cols in spread(down_ref.shape[1]):
        flipped_ref[cols, :] = jnp.transpose(down_ref[:, cols])


def flip(after, down):
    return pl.pallas_call(
        flip_kernel,
        in_specs=[REMOTE, WHOLE],
        out_specs=WHOLE,
        out_shape=pltpu.VMEM(down.shape[::-1], BF16),
        compiler_params=pltpu.CompilerParams(vmem_limit_bytes=8 * MIB),
        name="flip_down",
    )(*in_vmem(after, down))


def split_store(value, own_ref, other_ref, cols):
    half = own_ref.shape[0]
    own_ref[:, cols] = value[:half].astype(BF16)
    other_ref[:, cols] = value[half:].astype(BF16)


def forward_kernel(
    mine_ref, theirs_ref, gate_ref, up_ref, down_ref,
    own_ref, other_ref, hid_ref, gate_act_ref, up_act_ref, gate_flip_ref, up_flip_ref,
):
    gate_act = jnp.zeros(gate_act_ref.shape, F32)
    up_act = jnp.zeros(up_act_ref.shape, F32)
    for cols in spread(mine_ref.shape[1]):
        rows = jnp.concatenate([mine_ref[:, cols], theirs_ref[:, cols]], axis=0)
        gate_act = gate_act + matmul(rows, gate_ref[cols, :])
        up_act = up_act + matmul(rows, up_ref[cols, :])
        gate_flip_ref[:, cols] = jnp.transpose(gate_ref[cols, :])
    gate_act_ref[...] = gate_act
    up_act_ref[...] = up_act
    hidden = (gate_act * jax.nn.sigmoid(gate_act) * up_act).astype(BF16)
    hid_ref[...] = hidden
    for cols in spread(mine_ref.shape[1]):
        split_store(matmul(hidden, down_ref[:, cols]), own_ref, other_ref, cols)
        up_flip_ref[:, cols] = jnp.transpose(up_ref[cols, :])


def forward(mine, theirs, gate, up, down):
    half, depth = mine.shape
    width = gate.shape[1]
    return pl.pallas_call(
        forward_kernel,
        in_specs=[WHOLE] * 5,
        out_specs=[WHOLE] * 7,
        out_shape=[
            pltpu.VMEM((half, depth), BF16),
            pltpu.VMEM((half, depth), BF16),
            pltpu.VMEM((2 * half, width), BF16),
            pltpu.VMEM((2 * half, width), F32),
            pltpu.VMEM((2 * half, width), F32),
            pltpu.VMEM((width, depth), BF16),
            pltpu.VMEM((width, depth), BF16),
        ],
        compiler_params=pltpu.CompilerParams(vmem_limit_bytes=SCOPED),
        name="expert_forward",
    )(*in_vmem(mine, theirs, gate, up, down))


def row_grads(gate_cot, up_cot, gate_ref, up_ref, own_ref, other_ref, first):
    for j in range(own_ref.shape[1] // COLS):
        cols = pl.ds((first + j) * COLS, COLS)
        back = matmul(gate_cot, gate_ref[:, cols]) + matmul(up_cot, up_ref[:, cols])
        split_store(back, own_ref, other_ref, pl.ds(j * COLS, COLS))


def backward_kernel(
    mine_ref, theirs_ref, gate_ref, up_ref, down_ref, gate_act_ref, up_act_ref,
    own_ref, other_ref, gate_cot_ref, up_cot_ref,
):
    rows = jnp.concatenate([mine_ref[...], theirs_ref[...]], axis=0)
    hidden_cot = matmul(rows, down_ref[...])
    gate_act = gate_act_ref[...]
    sigma = jax.nn.sigmoid(gate_act)
    gate_cot = (hidden_cot * up_act_ref[...] * sigma * (1.0 + gate_act * (1.0 - sigma))).astype(BF16)
    up_cot = (hidden_cot * (gate_act * sigma)).astype(BF16)
    gate_cot_ref[...] = gate_cot
    up_cot_ref[...] = up_cot
    row_grads(gate_cot, up_cot, gate_ref, up_ref, own_ref, other_ref, 0)


def early_cols(depth):
    return depth // COLS * 4 // 7 * COLS


def backward(mine, theirs, gate, up, down, gate_act, up_act):
    half, depth = mine.shape
    width = gate.shape[0]
    early = early_cols(depth)
    return pl.pallas_call(
        backward_kernel,
        in_specs=[WHOLE] * 7,
        out_specs=[WHOLE] * 4,
        out_shape=[pltpu.VMEM((half, early), BF16)] * 2 + [pltpu.VMEM((2 * half, width), BF16)] * 2,
        compiler_params=pltpu.CompilerParams(vmem_limit_bytes=SCOPED),
        name="expert_backward",
    )(*in_vmem(mine, theirs, gate, up, down, gate_act, up_act))


def late_kernel(gate_cot_ref, up_cot_ref, gate_ref, up_ref, own_ref, other_ref):
    first = (gate_ref.shape[1] - own_ref.shape[1]) // COLS
    row_grads(gate_cot_ref[...], up_cot_ref[...], gate_ref, up_ref, own_ref, other_ref, first)


def late_rows(gate_cot, up_cot, gate, up):
    half = gate_cot.shape[0] // 2
    depth = gate.shape[1]
    late = depth - early_cols(depth)
    return pl.pallas_call(
        late_kernel,
        in_specs=[WHOLE] * 4,
        out_specs=[WHOLE] * 2,
        out_shape=[pltpu.VMEM((half, late), BF16)] * 2,
        compiler_params=pltpu.CompilerParams(vmem_limit_bytes=8 * MIB),
        name="late_rows",
    )(*in_vmem(gate_cot, up_cot, gate, up))


def add_columns(cap, first, own_out, arrived_out, own_ref, arrived_ref, out_ref):
    rows = out_ref.shape[0]
    groups = rows // (2 * cap)
    for here in spread(out_ref.shape[1]):
        cols = pl.ds(first + here.start, COLS)
        out = own_out[:, cols].astype(F32) + arrived_out[:, cols].astype(F32)
        grad = own_ref[:, here].astype(F32) + arrived_ref[:, here].astype(F32)
        both = jnp.concatenate([out.reshape(groups, cap, COLS), grad.reshape(groups, cap, COLS)], axis=1)
        out_ref[:, here] = both.reshape(rows, COLS).astype(BF16)


def add_early(cap, own_out, arrived_out, own, arrived):
    half, cols = own.shape
    return pl.pallas_call(
        lambda *refs: add_columns(cap, 0, *refs),
        in_specs=[WHOLE] * 4,
        out_specs=WHOLE,
        out_shape=pltpu.VMEM((2 * half, cols), BF16),
        compiler_params=pltpu.CompilerParams(vmem_limit_bytes=16 * MIB),
        name="add_early",
    )(*in_vmem(own_out, arrived_out, own, arrived))


def add_late_kernel(cap, early_ref, own_out, arrived_out, own_ref, arrived_ref, out_hbm, late_ref, sems):
    early = early_ref.shape[1]
    late = late_ref.shape[1]
    copy_early = pltpu.make_async_copy(early_ref, out_hbm.at[:, pl.ds(0, early)], sems.at[0])
    copy_early.start()
    add_columns(cap, early, own_out, arrived_out, own_ref, arrived_ref, late_ref)
    copy_late = pltpu.make_async_copy(late_ref, out_hbm.at[:, pl.ds(early, late)], sems.at[1])
    copy_late.start()
    copy_early.wait()
    copy_late.wait()


def add_late(cap, early, own_out, arrived_out, own, arrived):
    half, cols = own.shape
    depth = own_out.shape[1]
    return pl.pallas_call(
        lambda *refs: add_late_kernel(cap, *refs),
        in_specs=[WHOLE] * 5,
        out_specs=REMOTE,
        out_shape=pltpu.HBM((2 * half, depth), BF16),
        scratch_shapes=[pltpu.VMEM((2 * half, cols), BF16), pltpu.SemaphoreType.DMA((2,))],
        compiler_params=pltpu.CompilerParams(vmem_limit_bytes=16 * MIB),
        name="add_late",
    )(*in_vmem(early, own_out, arrived_out, own, arrived))


def grads_kernel(
    tok_mine, tok_theirs, cot_mine, cot_theirs, hid_ref, gate_cot_ref, up_cot_ref, gate_ref, up_ref, down_ref
):
    cols = pl.ds(pl.multiple_of(pl.program_id(0) * COLS, COLS), COLS)
    width = gate_ref.shape[1]
    pair = jnp.concatenate([gate_cot_ref[...], up_cot_ref[...]], axis=1)
    tokens = jnp.concatenate([tok_mine[:, cols], tok_theirs[:, cols]], axis=0)
    both = matmul(tokens, pair, ROWS_FIRST)
    gate_ref[...] = both[:, :width].astype(BF16)
    up_ref[...] = both[:, width:].astype(BF16)
    cotangent = jnp.concatenate([cot_mine[:, cols], cot_theirs[:, cols]], axis=0)
    down_ref[...] = matmul(hid_ref[...], cotangent, ROWS_FIRST).astype(BF16)


def grads(tok_mine, tok_theirs, cot_mine, cot_theirs, hidden, gate_cot, up_cot):
    depth = tok_mine.shape[1]
    width = hidden.shape[1]
    return pl.pallas_call(
        grads_kernel,
        grid=(depth // COLS,),
        in_specs=[WHOLE] * 7,
        out_specs=[
            pl.BlockSpec((COLS, width), lambda j: (j, 0)),
            pl.BlockSpec((COLS, width), lambda j: (j, 0)),
            pl.BlockSpec((width, COLS), lambda j: (0, j)),
        ],
        out_shape=[
            jax.ShapeDtypeStruct((depth, width), BF16),
            jax.ShapeDtypeStruct((depth, width), BF16),
            jax.ShapeDtypeStruct((width, depth), BF16),
        ],
        compiler_params=pltpu.CompilerParams(vmem_limit_bytes=SCOPED),
        name="weight_grads",
    )(*in_vmem(tok_mine, tok_theirs, cot_mine, cot_theirs, hidden, gate_cot, up_cot))


def combine_kernel(back_ref, select_ref, out_hbm, grad_hbm, out_ref, grad_ref, sems):
    count = out_ref.shape[0]
    copies = []
    for j, cols in enumerate(spread(back_ref.shape[1], COMBINE_COLS)):
        sums = matmul(select_ref[...], back_ref[:, cols])
        out_ref[:, cols] = (sums[:count] + sums[count : 2 * count]).astype(BF16)
        grad_ref[:, cols] = sums[2 * count :].astype(BF16)
        pair = [
            pltpu.make_async_copy(out_ref.at[:, cols], out_hbm.at[:, cols], sems.at[0, j]),
            pltpu.make_async_copy(grad_ref.at[:, cols], grad_hbm.at[:, cols], sems.at[1, j]),
        ]
        for copy in pair:
            copy.start()
        copies.extend(pair)
    for copy in copies:
        copy.wait()


def combine(back, select):
    width, depth = back.shape
    rows = select.shape[0] // 3
    return pl.pallas_call(
        combine_kernel,
        in_specs=[WHOLE, WHOLE],
        out_specs=[REMOTE, REMOTE],
        out_shape=[pltpu.HBM((rows, depth), BF16)] * 2,
        scratch_shapes=[
            pltpu.VMEM((rows, depth), BF16),
            pltpu.VMEM((rows, depth), BF16),
            pltpu.SemaphoreType.DMA((2, depth // COMBINE_COLS)),
        ],
        compiler_params=pltpu.CompilerParams(vmem_limit_bytes=8 * MIB),
        name="combine",
    )(*in_vmem(back), select)


def per_device(tokens, cotangent, expert_ids, route_weight, gate_weight, up_weight, down_weight):
    experts = lax.axis_size("ep")
    cap = tokens.shape[0] // 32
    depth = tokens.shape[1]
    swap = [(0, 1), (1, 0)]
    ids, weight = expert_ids.T, route_weight.T
    send = route(ids, weight, tokens, cotangent, experts, cap)
    select = selectors(ids, weight, experts, cap)

    orders = [list(range(experts)), [experts + (i ^ far_corner(experts)) for i in range(experts)]]

    def exchange(rows):
        blocks = rows.reshape(experts, 2 * cap, depth)
        return lax.all_to_all(
            blocks, ("edp", "ep"), split_axis=0, concat_axis=0, tiled=True, axis_index_groups=orders
        ).reshape(rows.shape)

    def swapped(rows, after=None):
        if after is not None:
            rows, after = lax.optimization_barrier((rows, after))
        return lax.ppermute(rows, "edp", swap), after

    gate, up, down = [
        lax.ppermute(w[0], "edp", swap) for w in (gate_weight, up_weight, down_weight)
    ]
    tok_mine, cot_mine = compact(exchange(send), cap)
    tok_theirs, _ = swapped(tok_mine)
    down_flip = flip(tok_mine, down)
    cot_theirs, _ = swapped(cot_mine)
    tok_theirs, down_flip = lax.optimization_barrier((tok_theirs, down_flip))
    own_out, other_out, hidden, gate_act, up_act, gate_flip, up_flip = forward(
        tok_mine, tok_theirs, gate, up, down
    )
    arrived_out, _ = swapped(other_out)
    own_early, other_early, gate_cot, up_cot = backward(
        cot_mine, cot_theirs, gate_flip, up_flip, down_flip, gate_act, up_act
    )
    arrived_early, _ = swapped(other_early)
    own_late, other_late = late_rows(gate_cot, up_cot, gate_flip, up_flip)
    arrived_late, _ = swapped(other_late)
    sums = add_early(cap, own_out, arrived_out, own_early, arrived_early)
    sums = add_late(cap, sums, own_out, arrived_out, own_late, arrived_late)
    back = exchange(sums)
    hidden, gate_cot, up_cot = [lax.ppermute(a, "edp", swap) for a in (hidden, gate_cot, up_cot)]
    grad_gate, grad_up, grad_down = grads(
        tok_theirs, tok_mine, cot_theirs, cot_mine, hidden, gate_cot, up_cot
    )
    routed_out, token_grad = combine(back, select)
    return (routed_out, token_grad, grad_gate[None], grad_up[None], grad_down[None])


def solution(mesh):
    in_specs = (
        P(("edp", "ep"), None),
        P(("edp", "ep"), None),
        P(("edp", "ep"), None),
        P(("edp", "ep"), None),
        P("ep", None, "edp"),
        P("ep", None, "edp"),
        P("ep", "edp", None),
    )
    out_specs = (
        P(("edp", "ep"), None),
        P(("edp", "ep"), None),
        P("ep", None, "edp"),
        P("ep", None, "edp"),
        P("ep", "edp", None),
    )
    return jax.shard_map(
        per_device, mesh=mesh, in_specs=in_specs, out_specs=out_specs, check_vma=False
    )
```

```python
import jax
import jax.numpy as jnp
from jax import lax
from jax.experimental import pallas as pl
from jax.experimental.pallas import tpu as pltpu
from jax.sharding import PartitionSpec as P

F32 = jnp.float32
BF16 = jnp.bfloat16
MIB = 1024 * 1024
SCOPED = 16 * MIB
ROWS_FIRST = (((0,), (0,)), ((), ()))
COLS = 512
ROUTE_COLS = 3584
COMBINE_COLS = 896


def matmul(a, b, dims=(((1,), (0,)), ((), ()))):
    return lax.dot_general(a, b, dims, preferred_element_type=F32)


WHOLE = pl.BlockSpec(memory_space=pltpu.VMEM)
REMOTE = pl.BlockSpec(memory_space=pl.ANY)


def spread(depth, size=COLS):
    return [pl.ds(j * size, size) for j in range(depth // size)]


def in_hbm(*arrays):
    return [pltpu.with_memory_space_constraint(a, pltpu.HBM) for a in arrays]


def in_vmem(*arrays):
    return [pltpu.with_memory_space_constraint(a, pltpu.VMEM) for a in arrays]


def far_corner(experts):
    return experts // 2 + experts // 8


def slots(cap, width, ids_ref, weight_ref, waits):
    tokens = ids_ref.shape[1]
    slot = lax.broadcasted_iota(jnp.int32, (width, tokens), 0)
    expert = (slot // (2 * cap)) ^ (lax.axis_index("edp") * far_corner(width // (2 * cap)))
    place = slot % (2 * cap)
    before = lax.broadcasted_iota(jnp.int32, (tokens, tokens), 0) < lax.broadcasted_iota(
        jnp.int32, (tokens, tokens), 1
    )
    before = jnp.where(before, 1.0, 0.0).astype(BF16)
    for copy in waits:
        copy.wait()
    member = jnp.zeros((width, tokens), F32)
    weight = jnp.zeros((width, tokens), F32)
    for k in range(ids_ref.shape[0]):
        hit = ids_ref[k : k + 1, :] == expert
        member = jnp.where(hit, 1.0, member)
        weight = jnp.where(hit, weight_ref[k : k + 1, :], weight)
    rank = matmul(member.astype(BF16), before)
    chosen = jnp.where(rank == (place % cap).astype(F32), member, 0.0)
    forward = jnp.where(place < cap, chosen, 0.0)
    return forward, chosen - forward, weight


def route_kernel(
    cap, ids_hbm, weight_hbm, tok_hbm, cot_hbm, send_ref, ids_ref, weight_ref, tok_ref, cot_ref, small_sems, sems
):
    parts = spread(tok_hbm.shape[1], ROUTE_COLS)
    small = [
        pltpu.make_async_copy(ids_hbm, ids_ref, small_sems.at[0]),
        pltpu.make_async_copy(weight_hbm, weight_ref, small_sems.at[1]),
    ]
    copies = [
        (
            pltpu.make_async_copy(tok_hbm.at[:, cols], tok_ref.at[:, cols], sems.at[0, j]),
            pltpu.make_async_copy(cot_hbm.at[:, cols], cot_ref.at[:, cols], sems.at[1, j]),
        )
        for j, cols in enumerate(parts)
    ]
    for copy in small:
        copy.start()
    for pair in copies:
        for copy in pair:
            copy.start()
    forward, backward, weight = slots(cap, send_ref.shape[0], ids_ref, weight_ref, small)
    scale = jnp.sum(forward + backward * weight, axis=1, keepdims=True)
    picks = jnp.concatenate([forward, backward], axis=1).astype(BF16)
    for pair, cols in zip(copies, parts):
        for copy in pair:
            copy.wait()
        rows = matmul(picks, jnp.concatenate([tok_ref[:, cols], cot_ref[:, cols]], axis=0))
        send_ref[:, cols] = (rows * scale).astype(BF16)


def route(ids, weight, tokens, cotangent, experts, cap):
    rows, depth = tokens.shape
    width = experts * 2 * cap
    return pl.pallas_call(
        lambda *refs: route_kernel(cap, *refs),
        in_specs=[REMOTE] * 4,
        out_specs=WHOLE,
        out_shape=pltpu.VMEM((width, depth), BF16),
        scratch_shapes=[
            pltpu.VMEM(ids.shape, jnp.int32),
            pltpu.VMEM(weight.shape, F32),
            pltpu.VMEM((rows, depth), BF16),
            pltpu.VMEM((rows, depth), BF16),
            pltpu.SemaphoreType.DMA((2,)),
            pltpu.SemaphoreType.DMA((2, depth // ROUTE_COLS)),
        ],
        compiler_params=pltpu.CompilerParams(vmem_limit_bytes=16 * MIB),
        name="route",
    )(*in_hbm(ids, weight, tokens, cotangent))


def select_kernel(cap, ids_hbm, weight_hbm, select_hbm, ids_ref, weight_ref, select_ref, sems):
    small = [
        pltpu.make_async_copy(ids_hbm, ids_ref, sems.at[0]),
        pltpu.make_async_copy(weight_hbm, weight_ref, sems.at[1]),
    ]
    for copy in small:
        copy.start()
    forward, backward, weight = slots(cap, select_ref.shape[1], ids_ref, weight_ref, small)
    weighted = jnp.transpose(forward * weight)
    high = weighted.astype(BF16)
    count = high.shape[0]
    select_ref[:count] = high
    select_ref[count : 2 * count] = (weighted - high.astype(F32)).astype(BF16)
    select_ref[2 * count :] = jnp.transpose(backward).astype(BF16)
    copy = pltpu.make_async_copy(select_ref, select_hbm, sems.at[2])
    copy.start()
    copy.wait()


def selectors(ids, weight, experts, cap):
    shape = (3 * ids.shape[1], experts * 2 * cap)
    return pl.pallas_call(
        lambda *refs: select_kernel(cap, *refs),
        in_specs=[REMOTE] * 2,
        out_specs=REMOTE,
        out_shape=jax.ShapeDtypeStruct(shape, BF16),
        scratch_shapes=[
            pltpu.VMEM(ids.shape, jnp.int32),
            pltpu.VMEM(weight.shape, F32),
            pltpu.VMEM(shape, BF16),
            pltpu.SemaphoreType.DMA((3,)),
        ],
        compiler_params=pltpu.CompilerParams(vmem_limit_bytes=8 * MIB),
        name="selectors",
    )(*in_hbm(ids, weight))


def compact_kernel(cap, rows_ref, early_ref, late_ref, cot_ref):
    groups = rows_ref.shape[0] // (2 * cap)
    half, early = early_ref.shape
    for j, cols in enumerate(spread(rows_ref.shape[1])):
        both = rows_ref[:, cols].astype(F32).reshape(groups, 2, cap, COLS)
        tok = both[:, 0].reshape(half, COLS).astype(BF16)
        if j * COLS < early:
            early_ref[:, cols] = tok
        else:
            late_ref[:, pl.ds(j * COLS - early, COLS)] = tok
        cot_ref[:, cols] = both[:, 1].reshape(half, COLS).astype(BF16)


def compact(rows, cap):
    half, depth = rows.shape[0] // 2, rows.shape[1]
    early = early_cols(depth)
    return pl.pallas_call(
        lambda *refs: compact_kernel(cap, *refs),
        in_specs=[WHOLE],
        out_specs=[WHOLE] * 3,
        out_shape=[pltpu.VMEM((half, w), BF16) for w in (early, depth - early, depth)],
        compiler_params=pltpu.CompilerParams(vmem_limit_bytes=8 * MIB),
        name="compact",
    )(*in_vmem(rows))


def flip_kernel(after_ref, down_ref, flipped_ref):
    for cols in spread(down_ref.shape[1]):
        flipped_ref[cols, :] = jnp.transpose(down_ref[:, cols])


def flip(after, down):
    return pl.pallas_call(
        flip_kernel,
        in_specs=[REMOTE, WHOLE],
        out_specs=WHOLE,
        out_shape=pltpu.VMEM(down.shape[::-1], BF16),
        compiler_params=pltpu.CompilerParams(vmem_limit_bytes=8 * MIB),
        name="flip_down",
    )(*in_vmem(after, down))


def split_store(value, own_ref, other_ref, cols):
    half = own_ref.shape[0]
    own_ref[:, cols] = value[:half].astype(BF16)
    other_ref[:, cols] = value[half:].astype(BF16)


def projections(mine_ref, theirs_ref, gate_ref, up_ref, first, gate_act, up_act, flips):
    for cols in spread(mine_ref.shape[1]):
        there = pl.ds(first + cols.start, COLS)
        rows = jnp.concatenate([mine_ref[:, cols], theirs_ref[:, cols]], axis=0)
        gate_act = gate_act + matmul(rows, gate_ref[there, :])
        up_act = up_act + matmul(rows, up_ref[there, :])
        flips[:, cols] = jnp.transpose(gate_ref[there, :])
    return gate_act, up_act


def begin_kernel(mine_ref, theirs_ref, gate_ref, up_ref, gate_act_ref, up_act_ref, gate_early_ref):
    zero = jnp.zeros(gate_act_ref.shape, F32)
    gate_act_ref[...], up_act_ref[...] = projections(
        mine_ref, theirs_ref, gate_ref, up_ref, 0, zero, zero, gate_early_ref
    )


def begin(mine, theirs, gate, up):
    half, early = mine.shape
    width = gate.shape[1]
    return pl.pallas_call(
        begin_kernel,
        in_specs=[WHOLE] * 4,
        out_specs=[WHOLE] * 3,
        out_shape=[pltpu.VMEM((2 * half, width), F32)] * 2 + [pltpu.VMEM((width, early), BF16)],
        compiler_params=pltpu.CompilerParams(vmem_limit_bytes=SCOPED),
        name="expert_begin",
    )(*in_vmem(mine, theirs, gate, up))


def forward_kernel(
    mine_ref, theirs_ref, gate_ref, up_ref, down_ref, gate_begun, up_begun,
    own_ref, other_ref, hid_ref, gate_act_ref, up_act_ref, gate_late_ref, up_early_ref,
):
    early = up_early_ref.shape[1]
    gate_act, up_act = projections(
        mine_ref, theirs_ref, gate_ref, up_ref, early, gate_begun[...], up_begun[...], gate_late_ref
    )
    gate_act_ref[...] = gate_act
    up_act_ref[...] = up_act
    hidden = (gate_act * jax.nn.sigmoid(gate_act) * up_act).astype(BF16)
    hid_ref[...] = hidden
    for j, cols in enumerate(spread(down_ref.shape[1])):
        split_store(matmul(hidden, down_ref[:, cols]), own_ref, other_ref, cols)
        if j * COLS < early:
            up_early_ref[:, cols] = jnp.transpose(up_ref[cols, :])


def forward(mine, theirs, gate, up, down, gate_begun, up_begun):
    half, late = mine.shape
    depth, width = gate.shape
    return pl.pallas_call(
        forward_kernel,
        in_specs=[WHOLE] * 7,
        out_specs=[WHOLE] * 7,
        out_shape=[
            pltpu.VMEM((half, depth), BF16),
            pltpu.VMEM((half, depth), BF16),
            pltpu.VMEM((2 * half, width), BF16),
            pltpu.VMEM((2 * half, width), F32),
            pltpu.VMEM((2 * half, width), F32),
            pltpu.VMEM((width, late), BF16),
            pltpu.VMEM((width, depth - late), BF16),
        ],
        compiler_params=pltpu.CompilerParams(vmem_limit_bytes=SCOPED),
        name="expert_forward",
    )(*in_vmem(mine, theirs, gate, up, down, gate_begun, up_begun))


def row_grads(gate_cot, up_cot, gate_ref, up_ref, own_ref, other_ref):
    for cols in spread(own_ref.shape[1]):
        back = matmul(gate_cot, gate_ref[:, cols]) + matmul(up_cot, up_ref[:, cols])
        split_store(back, own_ref, other_ref, cols)


def backward_kernel(
    mine_ref, theirs_ref, gate_early_ref, up_early_ref, up_ref, down_ref, gate_act_ref, up_act_ref,
    own_ref, other_ref, gate_cot_ref, up_cot_ref, up_late_ref,
):
    rows = jnp.concatenate([mine_ref[...], theirs_ref[...]], axis=0)
    hidden_cot = matmul(rows, down_ref[...])
    gate_act = gate_act_ref[...]
    sigma = jax.nn.sigmoid(gate_act)
    gate_cot = (hidden_cot * up_act_ref[...] * sigma * (1.0 + gate_act * (1.0 - sigma))).astype(BF16)
    up_cot = (hidden_cot * (gate_act * sigma)).astype(BF16)
    gate_cot_ref[...] = gate_cot
    up_cot_ref[...] = up_cot
    early = own_ref.shape[1]
    for cols in spread(up_late_ref.shape[1]):
        up_late_ref[:, cols] = jnp.transpose(up_ref[pl.ds(early + cols.start, COLS), :])
    row_grads(gate_cot, up_cot, gate_early_ref, up_early_ref, own_ref, other_ref)


def early_cols(depth):
    return depth // COLS * 4 // 7 * COLS


def backward(mine, theirs, gate_early, up_early, up, down, gate_act, up_act):
    half, depth = mine.shape
    width, early = gate_early.shape
    return pl.pallas_call(
        backward_kernel,
        in_specs=[WHOLE] * 8,
        out_specs=[WHOLE] * 5,
        out_shape=[pltpu.VMEM((half, early), BF16)] * 2
        + [pltpu.VMEM((2 * half, width), BF16)] * 2
        + [pltpu.VMEM((width, depth - early), BF16)],
        compiler_params=pltpu.CompilerParams(vmem_limit_bytes=SCOPED),
        name="expert_backward",
    )(*in_vmem(mine, theirs, gate_early, up_early, up, down, gate_act, up_act))


def late_kernel(gate_cot_ref, up_cot_ref, gate_ref, up_ref, own_ref, other_ref):
    row_grads(gate_cot_ref[...], up_cot_ref[...], gate_ref, up_ref, own_ref, other_ref)


def late_rows(gate_cot, up_cot, gate_late, up_late):
    half = gate_cot.shape[0] // 2
    late = gate_late.shape[1]
    return pl.pallas_call(
        late_kernel,
        in_specs=[WHOLE] * 4,
        out_specs=[WHOLE] * 2,
        out_shape=[pltpu.VMEM((half, late), BF16)] * 2,
        compiler_params=pltpu.CompilerParams(vmem_limit_bytes=8 * MIB),
        name="late_rows",
    )(*in_vmem(gate_cot, up_cot, gate_late, up_late))


def add_columns(cap, first, own_out, arrived_out, own_ref, arrived_ref, out_ref):
    rows = out_ref.shape[0]
    groups = rows // (2 * cap)
    for here in spread(out_ref.shape[1]):
        cols = pl.ds(first + here.start, COLS)
        out = own_out[:, cols].astype(F32) + arrived_out[:, cols].astype(F32)
        grad = own_ref[:, here].astype(F32) + arrived_ref[:, here].astype(F32)
        both = jnp.concatenate([out.reshape(groups, cap, COLS), grad.reshape(groups, cap, COLS)], axis=1)
        out_ref[:, here] = both.reshape(rows, COLS).astype(BF16)


def add_early(cap, own_out, arrived_out, own, arrived):
    half, cols = own.shape
    return pl.pallas_call(
        lambda *refs: add_columns(cap, 0, *refs),
        in_specs=[WHOLE] * 4,
        out_specs=WHOLE,
        out_shape=pltpu.VMEM((2 * half, cols), BF16),
        compiler_params=pltpu.CompilerParams(vmem_limit_bytes=16 * MIB),
        name="add_early",
    )(*in_vmem(own_out, arrived_out, own, arrived))


def add_late_kernel(cap, early_ref, own_out, arrived_out, own_ref, arrived_ref, out_hbm, late_ref, sems):
    early = early_ref.shape[1]
    late = late_ref.shape[1]
    copy_early = pltpu.make_async_copy(early_ref, out_hbm.at[:, pl.ds(0, early)], sems.at[0])
    copy_early.start()
    add_columns(cap, early, own_out, arrived_out, own_ref, arrived_ref, late_ref)
    copy_late = pltpu.make_async_copy(late_ref, out_hbm.at[:, pl.ds(early, late)], sems.at[1])
    copy_late.start()
    copy_early.wait()
    copy_late.wait()


def add_late(cap, early, own_out, arrived_out, own, arrived):
    half, cols = own.shape
    depth = own_out.shape[1]
    return pl.pallas_call(
        lambda *refs: add_late_kernel(cap, *refs),
        in_specs=[WHOLE] * 5,
        out_specs=REMOTE,
        out_shape=pltpu.HBM((2 * half, depth), BF16),
        scratch_shapes=[pltpu.VMEM((2 * half, cols), BF16), pltpu.SemaphoreType.DMA((2,))],
        compiler_params=pltpu.CompilerParams(vmem_limit_bytes=16 * MIB),
        name="add_late",
    )(*in_vmem(early, own_out, arrived_out, own, arrived))


def grads_kernel(
    tok_mine, tok_theirs, cot_mine, cot_theirs, hid_ref, gate_cot_ref, up_cot_ref, gate_ref, up_ref, down_ref
):
    cols = pl.ds(pl.multiple_of(pl.program_id(0) * COLS, COLS), COLS)
    width = gate_ref.shape[1]
    pair = jnp.concatenate([gate_cot_ref[...], up_cot_ref[...]], axis=1)
    tokens = jnp.concatenate([tok_mine[:, cols], tok_theirs[:, cols]], axis=0)
    both = matmul(tokens, pair, ROWS_FIRST)
    gate_ref[...] = both[:, :width].astype(BF16)
    up_ref[...] = both[:, width:].astype(BF16)
    cotangent = jnp.concatenate([cot_mine[:, cols], cot_theirs[:, cols]], axis=0)
    down_ref[...] = matmul(hid_ref[...], cotangent, ROWS_FIRST).astype(BF16)


def grads(tok_mine, tok_theirs, cot_mine, cot_theirs, hidden, gate_cot, up_cot):
    depth = tok_mine.shape[1]
    width = hidden.shape[1]
    return pl.pallas_call(
        grads_kernel,
        grid=(depth // COLS,),
        in_specs=[WHOLE] * 7,
        out_specs=[
            pl.BlockSpec((COLS, width), lambda j: (j, 0)),
            pl.BlockSpec((COLS, width), lambda j: (j, 0)),
            pl.BlockSpec((width, COLS), lambda j: (0, j)),
        ],
        out_shape=[
            jax.ShapeDtypeStruct((depth, width), BF16),
            jax.ShapeDtypeStruct((depth, width), BF16),
            jax.ShapeDtypeStruct((width, depth), BF16),
        ],
        compiler_params=pltpu.CompilerParams(vmem_limit_bytes=SCOPED),
        name="weight_grads",
    )(*in_vmem(tok_mine, tok_theirs, cot_mine, cot_theirs, hidden, gate_cot, up_cot))


def combine_kernel(back_ref, select_ref, out_hbm, grad_hbm, out_ref, grad_ref, sems):
    count = out_ref.shape[0]
    copies = []
    for j, cols in enumerate(spread(back_ref.shape[1], COMBINE_COLS)):
        sums = matmul(select_ref[...], back_ref[:, cols])
        out_ref[:, cols] = (sums[:count] + sums[count : 2 * count]).astype(BF16)
        grad_ref[:, cols] = sums[2 * count :].astype(BF16)
        pair = [
            pltpu.make_async_copy(out_ref.at[:, cols], out_hbm.at[:, cols], sems.at[0, j]),
            pltpu.make_async_copy(grad_ref.at[:, cols], grad_hbm.at[:, cols], sems.at[1, j]),
        ]
        for copy in pair:
            copy.start()
        copies.extend(pair)
    for copy in copies:
        copy.wait()


def combine(back, select):
    width, depth = back.shape
    rows = select.shape[0] // 3
    return pl.pallas_call(
        combine_kernel,
        in_specs=[WHOLE, WHOLE],
        out_specs=[REMOTE, REMOTE],
        out_shape=[pltpu.HBM((rows, depth), BF16)] * 2,
        scratch_shapes=[
            pltpu.VMEM((rows, depth), BF16),
            pltpu.VMEM((rows, depth), BF16),
            pltpu.SemaphoreType.DMA((2, depth // COMBINE_COLS)),
        ],
        compiler_params=pltpu.CompilerParams(vmem_limit_bytes=8 * MIB),
        name="combine",
    )(*in_vmem(back), select)


def per_device(tokens, cotangent, expert_ids, route_weight, gate_weight, up_weight, down_weight):
    experts = lax.axis_size("ep")
    cap = tokens.shape[0] // 32
    depth = tokens.shape[1]
    swap = [(0, 1), (1, 0)]
    ids, weight = expert_ids.T, route_weight.T
    send = route(ids, weight, tokens, cotangent, experts, cap)
    select = selectors(ids, weight, experts, cap)

    orders = [list(range(experts)), [experts + (i ^ far_corner(experts)) for i in range(experts)]]

    def exchange(rows):
        blocks = rows.reshape(experts, 2 * cap, depth)
        return lax.all_to_all(
            blocks, ("edp", "ep"), split_axis=0, concat_axis=0, tiled=True, axis_index_groups=orders
        ).reshape(rows.shape)

    def swapped(rows, after=None):
        if after is not None:
            rows, after = lax.optimization_barrier((rows, after))
        return lax.ppermute(rows, "edp", swap), after

    gate, up, down = [
        lax.ppermute(w[0], "edp", swap) for w in (gate_weight, up_weight, down_weight)
    ]
    early_mine, late_mine, cot_mine = compact(exchange(send), cap)
    early_theirs, _ = swapped(early_mine)
    late_theirs, _ = swapped(late_mine)
    down_flip = flip(early_mine, down)
    cot_theirs, _ = swapped(cot_mine)
    early_theirs, down_flip = lax.optimization_barrier((early_theirs, down_flip))
    gate_begun, up_begun, gate_early = begin(early_mine, early_theirs, gate, up)
    own_out, other_out, hidden, gate_act, up_act, gate_late, up_early = forward(
        late_mine, late_theirs, gate, up, down, gate_begun, up_begun
    )
    arrived_out, _ = swapped(other_out)
    own_early, other_early, gate_cot, up_cot, up_late = backward(
        cot_mine, cot_theirs, gate_early, up_early, up, down_flip, gate_act, up_act
    )
    arrived_early, _ = swapped(other_early)
    own_late, other_late = late_rows(gate_cot, up_cot, gate_late, up_late)
    arrived_late, _ = swapped(other_late)
    sums = add_early(cap, own_out, arrived_out, own_early, arrived_early)
    sums = add_late(cap, sums, own_out, arrived_out, own_late, arrived_late)
    back = exchange(sums)
    hidden, gate_cot, up_cot = [lax.ppermute(a, "edp", swap) for a in (hidden, gate_cot, up_cot)]
    tok_mine = jnp.concatenate([early_mine, late_mine], axis=1)
    tok_theirs = jnp.concatenate([early_theirs, late_theirs], axis=1)
    grad_gate, grad_up, grad_down = grads(
        tok_theirs, tok_mine, cot_theirs, cot_mine, hidden, gate_cot, up_cot
    )
    routed_out, token_grad = combine(back, select)
    return (routed_out, token_grad, grad_gate[None], grad_up[None], grad_down[None])


def solution(mesh):
    in_specs = (
        P(("edp", "ep"), None),
        P(("edp", "ep"), None),
        P(("edp", "ep"), None),
        P(("edp", "ep"), None),
        P("ep", None, "edp"),
        P("ep", None, "edp"),
        P("ep", "edp", None),
    )
    out_specs = (
        P(("edp", "ep"), None),
        P(("edp", "ep"), None),
        P("ep", None, "edp"),
        P("ep", None, "edp"),
        P("ep", "edp", None),
    )
    return jax.shard_map(
        per_device, mesh=mesh, in_specs=in_specs, out_specs=out_specs, check_vma=False
    )
```
